32 devices in a mesh: panel: 2 (over core), ang: 4 (over z), rad: 4 (over y, x).
Axes of the slice: x: 2, y: 2, z: 4, core: 2. Of those that a mesh axis runs over, the one named last changes fastest.
Arguments:
- density: float32 [2, 8, 64, 512], P('panel', 'rad', 'ang'), may hold values from 1 to 2
- momentum: float32 [2, 3, 8, 64, 512], P('panel', None, 'rad', 'ang'), may hold values from -2.5 to 2.5
- magnetic: float32 [2, 3, 8, 64, 512], P('panel', None, 'rad', 'ang'), may hold values from -2.5 to 2.5
- partner_device: int32 [2, 128, 1], P('panel', 'ang'), may hold values from 0 to 3; in each aligned block of 32 rows (0 to 31, 32 to 63, ..., all dimensions but the last counted through in order) at most 16 rows name the same one
- partner_phi: int32 [2, 128], P('panel', 'ang'), may hold values from 0 to 14
- partner_theta: int32 [2, 128], P('panel', 'ang'), may hold values from 0 to 510
- partner_weight: float32 [2, 128, 4], P('panel', 'ang'), may hold values from 0 to 1, as said below
- border_turn: float32 [2, 128], P('panel', 'ang'), may hold values from -3.140625 to 3.140625
Outputs:
- density_next: float32 [2, 8, 64, 512], P('panel', 'rad', 'ang')
- momentum_next: float32 [2, 3, 8, 64, 512], P('panel', None, 'rad', 'ang')
- magnetic_next: float32 [2, 3, 8, 64, 512], P('panel', None, 'rad', 'ang')
The draws below stay inside these ranges and needn't reach their ends.
Inputs may be any that keep to these rules, and one draw needn't show every extreme that they name: `partner_device`: within the 32 table rows of one device (aligned blocks), at most 16 rows name the same source device. `partner_weight`: each row's weights are (1-u)(1-v), (1-u)v, u(1-v), uv for some u, v in [0, 1].
All inputs are finite; a program needn't handle non-finite values.
Results may differ from the reference program's by a relative error of at most 0.00005.
Values sent between devices are 32-bit elements; how exact they have to be, the bound alone decides.
A program may use at most 64 MiB of HBM per device.

```python
import math
import jax
import jax.numpy as jnp
import numpy as np

CP = 16
NT = 512
PANELS = 2
NR = 8
NP = 64
BORDER = 32
ANG_ROWS = 128
MOST = 16
N_ANG = 4


def draw_partner_weight(key, part):
    first_key, second_key = jax.random.split(jax.random.fold_in(key, 17))
    along_phi = jax.random.uniform(first_key, (PANELS, ANG_ROWS), jnp.float32)
    along_theta = jax.random.uniform(second_key, (PANELS, ANG_ROWS), jnp.float32)
    return jnp.stack([(1.0 - along_phi) * (1.0 - along_theta), (1.0 - along_phi) * along_theta, along_phi * (1.0 - along_theta), along_phi * along_theta], axis=-1)


def with_ends(values, rng, least, high):
    index_at = [jax.random.randint(jax.random.fold_in(rng, axis), (), 0, length) for axis, length in enumerate(values.shape)]
    main_axis = values.shape.index(max(values.shape))
    next_to = index_at[:main_axis] + [(index_at[main_axis] + 1) % values.shape[main_axis]] + index_at[main_axis + 1:]
    return values.at[tuple(index_at)].set(least).at[tuple(next_to)].set(high)


def steps_of(key, dims, cuts, low, top_value):
    loudness = 1.0
    for axis_at, parts in cuts:
        steps = jax.random.uniform(jax.random.fold_in(jax.random.fold_in(key, 6), axis_at), (parts,), jnp.float32, low / len(cuts), top_value / len(cuts))
        loudness = loudness * jnp.repeat(jnp.exp(steps), dims[axis_at] // parts).reshape((-1,) + (1,) * (len(dims) - 1 - axis_at))
    return loudness


def shared_out(own_key, own, number, rows, amount, top, limit, skew):
    sequence = jax.random.permutation(own_key, amount)
    crowded, ordinary = portions_of(amount, rows * top, limit, skew, True), portions_of(amount, rows * top, limit, skew, False)
    places = jnp.arange(amount)

    def named(sizes, rotation):
        used = int((sizes > 0).sum())
        fixed = max(1, used // 4)
        passed = fixed + (places - fixed + rotation * (used - fixed)) % max(1, amount - fixed)
        return jnp.zeros((amount,), jnp.int32).at[sequence[jnp.where(places < fixed, places, passed)]].set(jnp.asarray(sizes, jnp.int32))

    sizes = jnp.where(number % 4 == 0, named(crowded, number // 4), named(ordinary, number - number // 4 - 1))
    mixed = jax.random.permutation(jax.random.fold_in(own, 3), amount)
    donor, receiver = mixed[0:amount // 2 * 2:2], mixed[1:amount // 2 * 2:2]
    slack = jnp.minimum(sizes[donor] - 1, limit - sizes[receiver]) // 2
    slack = jnp.where((donor == sequence[0]) | (receiver == sequence[0]) | (sizes[receiver] == 0), 0, jnp.maximum(slack, 0))
    passed = jax.random.randint(jax.random.fold_in(own, 4), (amount // 2,), 0, 1 << 20) % (slack + 1)
    sizes = sizes.at[donor].add(-passed).at[receiver].add(passed)
    members = jnp.searchsorted(jnp.cumsum(sizes), jnp.arange(rows * top), side="right").astype(jnp.int32)
    listing = members.reshape(top, rows).T
    listing = listing[jax.random.permutation(jax.random.fold_in(own, 1), rows)]
    rotation = jax.random.randint(jax.random.fold_in(own, 2), (rows, 1), 0, top)
    return jnp.take_along_axis(listing, (jnp.arange(top)[None, :] + rotation) % top, axis=1)


def portions_of(count, total, bound, slope, full):
    weights = [(1 << 20) // math.isqrt(standing ** slope) + 1 for standing in range(1, count + 1)]
    largest = bound if full else min(bound, max(-(-total // count), total * weights[0] // sum(weights)))
    least = 1 if total - largest >= count - 1 else 0
    holding, spare = [largest] + [least] * (count - 1), total - largest - least * (count - 1)
    while spare > 0:
        candidates = [i for i in range(1, count) if holding[i] < largest] or [i for i in range(1, count) if holding[i] < bound]
        whole, remaining = sum([weights[i] for i in candidates]), spare
        for i in candidates:
            more = min(bound - holding[i], max(1, remaining * weights[i] // whole), spare)
            holding[i] = holding[i] + more
            spare = spare - more
    return np.array(holding)


def normal_values(stream_key, shape, scale, limit, cuts=(), kind=jnp.bfloat16):
    values = scale * jax.random.normal(stream_key, shape, jnp.float32)
    if cuts:
        values = values * steps_of(stream_key, shape, cuts, -0.22, 0.18)
    return jnp.clip(values, -limit, limit).astype(kind)


def setup_inputs(seed: int = 0) -> dict:
    keys = jax.random.split(jax.random.key(seed), 9)
    density = jnp.clip(1.0 + 1.0 * jax.random.uniform(keys[0], (PANELS, NR, NP, NT), jnp.float32) ** steps_of(keys[0], (PANELS, NR, NP, NT), ((0, 2), (1, 4), (2, 4)), -0.2, 0.2), 1.0, 2.0)
    momentum = normal_values(keys[1], (PANELS, 3, NR, NP, NT), 0.3, 2.5, ((0, 2), (2, 4), (3, 4)), jnp.float32)
    magnetic = normal_values(keys[2], (PANELS, 3, NR, NP, NT), 0.4, 2.5, ((0, 2), (2, 4), (3, 4)), jnp.float32)
    partner_device_keys = jax.random.split(jax.random.fold_in(keys[3], 1), PANELS * ANG_ROWS // BORDER)
    partner_device_turns = jax.random.permutation(jax.random.fold_in(keys[3], 3), PANELS * ANG_ROWS // BORDER)
    partner_device = jax.vmap(lambda own, number: shared_out(jax.random.fold_in(keys[3], 2), own, number, BORDER, N_ANG, 1, MOST, 2))(partner_device_keys, partner_device_turns).reshape((PANELS, ANG_ROWS, 1))
    partner_phi = with_ends(jax.random.randint(keys[4], (PANELS, ANG_ROWS), 0, CP - 1), jax.random.fold_in(keys[4], 1), 0, (CP - 1) - 1).astype(jnp.int32)
    partner_theta = with_ends(jax.random.randint(keys[5], (PANELS, ANG_ROWS), 0, NT - 1), jax.random.fold_in(keys[5], 1), 0, (NT - 1) - 1).astype(jnp.int32)
    partner_weight = draw_partner_weight(jax.random.fold_in(keys[8], 71), 0)
    border_turn = jnp.clip(jax.random.uniform(keys[7], (PANELS, ANG_ROWS), jnp.float32, -3.140625, 3.140625), -3.140625, 3.140625)
    return dict(density=density, momentum=momentum, magnetic=magnetic, partner_device=partner_device, partner_phi=partner_phi, partner_theta=partner_theta, partner_weight=partner_weight, border_turn=border_turn)


time_step = 0.15
sound_sq = 1.0
viscosity = 0.1
resistivity = 0.1
r_inner = 0.35
corner_steps = ((0, 0), (0, 1), (1, 0), (1, 1))


def field_of(block, index):
    return block[..., index, :, :, :]


def fluxes(block, direction):
    mass_field = field_of(block, 0)
    moment = [field_of(block, 1 + component) for component in range(3)]
    magnet = [field_of(block, 4 + component) for component in range(3)]
    velocity = [moment[component] / mass_field for component in range(3)]
    pressure = sound_sq * mass_field + 0.5 * (magnet[0] * magnet[0] + magnet[1] * magnet[1] + magnet[2] * magnet[2])
    pieces = [moment[direction]]
    for component in range(3):
        flux_term = moment[component] * velocity[direction] - magnet[component] * magnet[direction]
        if component == direction:
            flux_term = flux_term + pressure
        pieces.append(flux_term)
    for component in range(3):
        pieces.append(velocity[direction] * magnet[component] - magnet[direction] * velocity[component])
    return jnp.stack(pieces, axis=-4)


def tendency(current, radial, polar, azimuth, half_t, half_p, sq_t, sq_p):
    flux_r = fluxes(radial, 0)
    flux_t = fluxes(polar, 1)
    flux_p = fluxes(azimuth, 2)
    divergence = (flux_r[..., 2:, :, :] - flux_r[..., :-2, :, :]) * 0.5
    divergence = divergence + (flux_t[..., 2:] - flux_t[..., :-2]) * half_t
    divergence = divergence + (flux_p[..., :, 2:, :] - flux_p[..., :, :-2, :]) * half_p
    laplace_sum = radial[..., 2:, :, :] - 2.0 * current + radial[..., :-2, :, :]
    laplace_sum = laplace_sum + (polar[..., 2:] - 2.0 * current + polar[..., :-2]) * sq_t
    laplace_sum = laplace_sum + (azimuth[..., :, 2:, :] - 2.0 * current + azimuth[..., :, :-2, :]) * sq_p
    mixing = jnp.array([0.0, viscosity, viscosity, viscosity, resistivity, resistivity, resistivity], jnp.float32).reshape(7, 1, 1, 1)
    return mixing * laplace_sum - divergence


def turn_frame(ghost, cosine, sine):
    pieces = [ghost[0], ghost[1]]
    pieces.append(cosine * ghost[2] + sine * ghost[3])
    pieces.append(cosine * ghost[3] - sine * ghost[2])
    pieces.append(ghost[4])
    pieces.append(cosine * ghost[5] + sine * ghost[6])
    pieces.append(cosine * ghost[6] - sine * ghost[5])
    return jnp.stack(pieces, axis=0)


def reference(density, momentum, magnetic, partner_device, partner_phi, partner_theta, partner_weight, border_turn):
    fields_now = jnp.concatenate([density[:, None], momentum, magnetic], axis=1)
    radius = r_inner + (jnp.arange(NR).astype(jnp.float32) + 0.5) * ((1.0 - r_inner) / NR)
    colatitude = math.pi / 4 + (jnp.arange(NT).astype(jnp.float32) + 0.5) * (math.pi / 2 / NT)
    inv_radius = (1.0 / radius).reshape(NR, 1, 1)
    inv_both = inv_radius / jnp.sin(colatitude)
    half_t = 0.5 * inv_radius
    half_p = 0.5 * inv_both
    sq_t = inv_radius * inv_radius
    sq_p = inv_both * inv_both
    mirror = jnp.array([1.0, -1.0, -1.0, -1.0, 1.0, 1.0, 1.0], jnp.float32).reshape(7, 1, 1, 1)
    phi_start = partner_device[..., 0] * CP + partner_phi

    def overset(current):
        lowers = []
        uppers = []
        for panel_side in range(2):
            source_grid = current[1 - panel_side]
            phi_base = phi_start[panel_side]
            theta_base = partner_theta[panel_side]
            weights = partner_weight[panel_side]
            values = [source_grid[:, :, phi_base + step_phi, theta_base + step_theta] for step_phi, step_theta in corner_steps]
            ghost = weights[:, 0] * values[0] + weights[:, 1] * values[1]
            ghost = ghost + weights[:, 2] * values[2]
            ghost = ghost + weights[:, 3] * values[3]
            angle = border_turn[panel_side]
            ghost = turn_frame(ghost, jnp.cos(angle), jnp.sin(angle))
            ghost = ghost.reshape(7, NR, N_ANG, 2, CP)
            lowers.append(ghost[:, :, :, 0, :].reshape(7, NR, NP))
            uppers.append(ghost[:, :, :, 1, :].reshape(7, NR, NP))
        return jnp.stack(lowers, axis=0), jnp.stack(uppers, axis=0)

    def evaluate(current):
        radial = jnp.concatenate([mirror * current[:, :, :1], current, mirror * current[:, :, -1:]], axis=2)
        azimuth = jnp.concatenate([mirror * current[:, :, :, :1], current, mirror * current[:, :, :, -1:]], axis=3)
        lower_t, upper_t = overset(current)
        polar = jnp.concatenate([lower_t[..., None], current, upper_t[..., None]], axis=4)
        return tendency(current, radial, polar, azimuth, half_t, half_p, sq_t, sq_p)

    slope_one = evaluate(fields_now)
    slope_two = evaluate(fields_now + (0.5 * time_step) * slope_one)
    slope_three = evaluate(fields_now + (0.5 * time_step) * slope_two)
    slope_four = evaluate(fields_now + time_step * slope_three)
    updated = fields_now + (time_step / 6.0) * (slope_one + 2.0 * slope_two + 2.0 * slope_three + slope_four)
    return updated[:, 0], updated[:, 1:4], updated[:, 4:7]
```

```python
import functools
import math

import jax
import jax.numpy as jnp
from jax import lax
from jax.experimental import pallas as pl
from jax.experimental.pallas import tpu as pltpu
from jax.sharding import PartitionSpec as P

time_step = 0.15
mixing = (0.0, 0.1, 0.1, 0.1, 0.1, 0.1, 0.1)
wall = (1.0, -1.0, -1.0, -1.0, 1.0, 1.0, 1.0)
r_inner = 0.35
FIELDS = 7
LANES = 128
LEVELS = 8
ahead = (0.5 * time_step, 0.5 * time_step, time_step)
share = (time_step / 6.0, time_step / 3.0, time_step / 3.0, time_step / 6.0)


def point_values(u):
    rate = 1.0 / u[0]
    speed = [u[1 + c] * rate for c in range(3)]
    pressure = u[0] + 0.5 * (u[4] * u[4] + u[5] * u[5] + u[6] * u[6])
    return speed, pressure


def flux_of(u, speed, pressure, d, stress, twist):
    out = [u[1 + d]]
    for c in range(3):
        key = (min(c, d), max(c, d))
        if key not in stress:
            term = u[1 + c] * speed[d] - u[4 + c] * u[4 + d]
            stress[key] = term + pressure if c == d else term
        out.append(stress[key])
    for c in range(3):
        if c == d:
            out.append(None)
            continue
        key = (min(c, d), max(c, d))
        if key not in twist:
            low, high = key
            twist[key] = speed[high] * u[4 + low] - u[4 + high] * speed[low]
        out.append(twist[key] if c == key[0] else -twist[key])
    return out


def low_high(u, flux, half, mix):
    low, high = [], []
    for f in range(FIELDS):
        carried = None if flux[f] is None else half * flux[f]
        spread = None if mixing[f] == 0.0 else mix * u[f]
        if carried is None:
            low.append(spread)
            high.append(spread)
        elif spread is None:
            low.append(carried)
            high.append(-carried)
        else:
            low.append(spread + carried)
            high.append(spread - carried)
    return low, high


def kernel(
    sizes,
    den, mom, mag, pdev, pphi, ptheta, pweight, pturn,
    oden, omom, omag,
    land, staged, state, total, slope, x_low, x_high, geo,
    phi_in, theta_out, theta_in, over_out, over_in,
    meta_out, meta_in, coef, picker,
    own_sem, load_send, load_recv, give_send, give_recv,
    meta_send, meta_recv, phi_send, phi_recv, theta_send, theta_recv,
    over_send, over_recv,
):
    n_ang, n_rad, rows, cells, border = sizes
    side_rows = border // 2
    per_tile = LANES // border
    tiles = n_ang // per_tile
    sources = n_ang * n_rad
    mine = lax.axis_index("panel")
    a = lax.axis_index("ang")
    t = lax.axis_index("rad")
    other = 1 - mine

    def at(panel, ang, rad):
        return {"panel": panel, "ang": ang, "rad": rad}

    barrier = pltpu.get_barrier_semaphore()

    def greet(i, carry):
        pl.semaphore_signal(
            barrier, inc=1,
            device_id=at(other, i // n_rad, lax.rem(i, n_rad)),
            device_id_type=pl.DeviceIdType.MESH,
        )
        return carry

    lax.fori_loop(0, sources, greet, 0)
    for step in range(1, n_rad):
        pl.semaphore_signal(
            barrier, inc=1, device_id=at(mine, a, lax.rem(t + step, n_rad)),
            device_id_type=pl.DeviceIdType.MESH,
        )

    @pl.when(a > 0)
    def _():
        pl.semaphore_signal(
            barrier, inc=1, device_id=at(mine, a - 1, t), device_id_type=pl.DeviceIdType.MESH
        )

    @pl.when(a < n_ang - 1)
    def _():
        pl.semaphore_signal(
            barrier, inc=1, device_id=at(mine, a + 1, t), device_id_type=pl.DeviceIdType.MESH
        )

    own_rows = pl.ds(pl.multiple_of(t * rows, rows), rows)
    own_lanes = pl.ds(pl.multiple_of(t * LANES, LANES), LANES)
    own = [
        pltpu.make_async_copy(den.at[:, own_lanes], land.at[0, own_rows, :], own_sem.at[0]),
        pltpu.make_async_copy(mom.at[:, :, own_lanes], land.at[pl.ds(1, 3), own_rows, :], own_sem.at[1]),
        pltpu.make_async_copy(mag.at[:, :, own_lanes], land.at[pl.ds(4, 3), own_rows, :], own_sem.at[2]),
    ]
    for copy in own:
        copy.start()

    sub8 = lax.broadcasted_iota(jnp.int32, (LEVELS, LANES), 0)
    lane8 = lax.broadcasted_iota(jnp.int32, (LEVELS, LANES), 1)
    sub_b = lax.broadcasted_iota(jnp.int32, (border, LANES), 0)
    lane_b = lax.broadcasted_iota(jnp.int32, (border, LANES), 1)
    square = (
        lax.broadcasted_iota(jnp.int32, (border, border), 0)
        == lax.broadcasted_iota(jnp.int32, (border, border), 1)
    )

    def column(row):
        wide = jnp.broadcast_to(row, (border, border))
        return jnp.sum(jnp.where(square, wide, 0.0), axis=1, keepdims=True)

    place = lane_b == sub_b + border * lax.rem(a, per_tile)
    columns = [
        pdev[...].astype(jnp.float32),
        column(pphi[...].astype(jnp.float32)),
        column(ptheta[...].astype(jnp.float32)),
    ] + [pweight[:, i:i + 1] for i in range(4)]
    meta_out[...] = jnp.zeros_like(meta_out)
    for i, col in enumerate(columns):
        meta_out[i:i + 1, :] = jnp.sum(
            jnp.where(place, jnp.broadcast_to(col, (border, LANES)), 0.0), axis=0, keepdims=True
        )

    at_low = t == 0
    at_high = t == n_rad - 1
    base_row = jnp.where(at_high, side_rows, 0)
    turn_at = sub_b == base_row + lax.rem(lane_b, side_rows)
    angle = jnp.sum(
        jnp.where(turn_at, jnp.broadcast_to(column(pturn[...]), (border, LANES)), 0.0),
        axis=0, keepdims=True,
    )
    angle = jnp.broadcast_to(angle, (LEVELS, LANES))
    cosine, sine = jnp.cos(angle), jnp.sin(angle)

    radius = r_inner + (sub8.astype(jnp.float32) + 0.5) * ((1.0 - r_inner) / LEVELS)
    theta = math.pi / 4 + ((lane8 + t * LANES).astype(jnp.float32) + 0.5) * (
        math.pi / 2 / (LANES * n_rad)
    )
    inv_radius = 1.0 / radius
    inv_both = inv_radius / jnp.sin(theta)
    half_t = 0.5 * inv_radius
    mix_t = 0.1 * inv_radius * inv_radius
    half_p = 0.5 * inv_both
    mix_p = 0.1 * inv_both * inv_both
    centre = -2.0 * (0.1 + mix_t + mix_p)
    for i, value in enumerate((half_t, mix_t, half_p, mix_p, centre)):
        geo[i] = value

    pl.semaphore_wait(
        barrier,
        sources + n_rad - 1 + jnp.where(a > 0, 1, 0) + jnp.where(a < n_ang - 1, 1, 0),
    )

    loads = []
    for step in range(1, n_rad):
        to = lax.rem(t + step, n_rad)
        lanes = pl.ds(pl.multiple_of(to * LANES, LANES), LANES)
        for i, (src, dst) in enumerate((
            (den.at[:, lanes], land.at[0, own_rows, :]),
            (mom.at[:, :, lanes], land.at[pl.ds(1, 3), own_rows, :]),
            (mag.at[:, :, lanes], land.at[pl.ds(4, 3), own_rows, :]),
        )):
            loads.append(pltpu.make_async_remote_copy(
                src_ref=src, dst_ref=dst,
                send_sem=load_send.at[i, step], recv_sem=load_recv.at[i, step],
                device_id=at(mine, a, to), device_id_type=pl.DeviceIdType.MESH,
            ))
    for copy in loads:
        copy.start()

    def meta_copy(to):
        return pltpu.make_async_remote_copy(
            src_ref=meta_out, dst_ref=meta_in.at[a],
            send_sem=meta_send, recv_sem=meta_recv,
            device_id=at(other, to, t), device_id_type=pl.DeviceIdType.MESH,
        )

    def send_meta(to, carry):
        meta_copy(to).start()
        return carry

    lax.fori_loop(0, n_ang, send_meta, 0)
    pltpu.make_async_copy(meta_in, meta_in, meta_recv).wait()

    sub_l = lax.broadcasted_iota(jnp.int32, (LANES, LANES), 0)
    sub_c = lax.broadcasted_iota(jnp.int32, (cells, LANES), 0)

    def prepare(g, carry):
        table = jnp.sum(meta_in[pl.ds(g * per_tile, per_tile)], axis=0)
        device = table[0:1].astype(jnp.int32)
        at_phi = table[1:2].astype(jnp.int32)
        at_theta = table[2:3].astype(jnp.int32) - t * LANES
        hit = jnp.broadcast_to(device == a, (cells, LANES))
        near = hit & (sub_c == at_phi)
        far = hit & (sub_c == at_phi + 1)
        zero = jnp.zeros((cells, LANES), jnp.float32)
        w = [jnp.broadcast_to(table[3 + i:4 + i], (cells, LANES)) for i in range(4)]
        coef[g, 0] = jnp.where(near, w[0], jnp.where(far, w[2], zero))
        coef[g, 1] = jnp.where(near, w[1], jnp.where(far, w[3], zero))
        first = jnp.where(sub_l == at_theta, 1.0, 0.0).astype(jnp.bfloat16)
        second = jnp.where(sub_l == at_theta + 1, 1.0, 0.0).astype(jnp.bfloat16)
        for part in range(2):
            picker[g, pl.ds(part * LANES, LANES), pl.ds(0, LANES)] = first
            picker[g, pl.ds(part * LANES, LANES), pl.ds(LANES, LANES)] = second
        return carry

    if tiles == 1:
        prepare(0, 0)
    else:
        lax.fori_loop(0, tiles, prepare, 0)

    for copy in own:
        copy.wait()
    for copy in loads:
        copy.wait_recv()

    block_of = lane8 // side_rows
    first_lane = lane8 == 0
    last_lane = lane8 == LANES - 1
    first_level = sub8 == 0
    last_level = sub8 == LEVELS - 1

    def pack(k, f, value, packs):
        low, high = packs
        spot = f * cells + k
        hit = lane8 == spot
        low = jnp.where(hit, pltpu.roll(value, spot, 1), low)
        high = jnp.where(hit, pltpu.roll(value, spot + 1, 1), high)
        return low, high

    def phi_copies(s):
        down = pltpu.make_async_remote_copy(
            src_ref=state.at[s, 0], dst_ref=phi_in.at[s, 1],
            send_sem=phi_send.at[s, 0], recv_sem=phi_recv.at[s, 1],
            device_id=at(mine, a, t) | {"ang": jnp.maximum(a - 1, 0)},
            device_id_type=pl.DeviceIdType.MESH,
        )
        up = pltpu.make_async_remote_copy(
            src_ref=state.at[s, cells - 1], dst_ref=phi_in.at[s, 0],
            send_sem=phi_send.at[s, 1], recv_sem=phi_recv.at[s, 0],
            device_id=at(mine, a, t) | {"ang": jnp.minimum(a + 1, n_ang - 1)},
            device_id_type=pl.DeviceIdType.MESH,
        )
        return down, up

    def theta_copies(s):
        down = pltpu.make_async_remote_copy(
            src_ref=theta_out.at[s, 0], dst_ref=theta_in.at[s, 1],
            send_sem=theta_send.at[s, 0], recv_sem=theta_recv.at[s, 1],
            device_id=at(mine, a, jnp.maximum(t - 1, 0)),
            device_id_type=pl.DeviceIdType.MESH,
        )
        up = pltpu.make_async_remote_copy(
            src_ref=theta_out.at[s, 1], dst_ref=theta_in.at[s, 0],
            send_sem=theta_send.at[s, 1], recv_sem=theta_recv.at[s, 0],
            device_id=at(mine, a, jnp.minimum(t + 1, n_rad - 1)),
            device_id_type=pl.DeviceIdType.MESH,
        )
        return down, up

    def over_copy(s, q):
        return pltpu.make_async_remote_copy(
            src_ref=over_out.at[s, q], dst_ref=over_in.at[s, a * n_rad + t],
            send_sem=over_send.at[s], recv_sem=over_recv.at[s],
            device_id=at(other, q // 2, lax.rem(q, 2) * (n_rad - 1)),
            device_id_type=pl.DeviceIdType.MESH,
        )

    def send_all(s, packs):
        theta_out[s, 0], theta_out[s, 1] = packs
        theta_down, theta_up = theta_copies(s)
        phi_down, phi_up = phi_copies(s)
        for can, copy in (
            (t > 0, theta_down), (t < n_rad - 1, theta_up),
            (a > 0, phi_down), (a < n_ang - 1, phi_up),
        ):
            pl.when(can)(copy.start)

        def overset(g, carry):
            turned = []
            for f in range(FIELDS):
                value = state[s, :, f].reshape(cells * LEVELS, LANES)
                head = value.astype(jnp.bfloat16)
                rest = (value - head.astype(jnp.float32)).astype(jnp.bfloat16)
                got = jnp.dot(
                    jnp.concatenate([head, rest], axis=1), picker[g],
                    preferred_element_type=jnp.float32,
                )
                ghost = None
                for k in range(cells):
                    piece = got[k * LEVELS:(k + 1) * LEVELS]
                    term = (
                        piece[:, :LANES] * coef[g, 0, k:k + 1, :]
                        + piece[:, LANES:] * coef[g, 1, k:k + 1, :]
                    )
                    ghost = term if ghost is None else ghost + term
                turned.append(pltpu.roll(ghost, f * side_rows, 1) if f else ghost)
            groups = LANES // side_rows
            for j in range(groups):
                message = turned[0]
                for f in range(FIELDS):
                    message = jnp.where(block_of == (f + j) % groups, turned[f], message)
                if j:
                    message = pltpu.roll(message, LANES - j * side_rows, 1)
                over_out[s, g * groups + j] = message
            for j in range(groups):
                over_copy(s, g * groups + j).start()
            return carry

        if tiles == 1:
            overset(0, 0)
        else:
            lax.fori_loop(0, tiles, overset, 0)

    def inner(s):
        half_t, mix_t, half_p, mix_p, centre = [geo[i] for i in range(5)]

        def row(k, carry):
            u = [state[s, k, f] for f in range(FIELDS)]
            speed, pressure = point_values(u)
            stress, twist = {}, {}
            low_r, high_r = low_high(u, flux_of(u, speed, pressure, 0, stress, twist), 0.5, 0.1)
            low_t, high_t = low_high(u, flux_of(u, speed, pressure, 1, stress, twist), half_t, mix_t)
            low_p, high_p = low_high(u, flux_of(u, speed, pressure, 2, stress, twist), half_p, mix_p)
            for f in range(FIELDS):
                below = pltpu.roll(low_r[f], 1, 0)
                above = pltpu.roll(high_r[f], LEVELS - 1, 0)
                below = jnp.where(first_level, wall[f] * high_r[f], below)
                above = jnp.where(last_level, wall[f] * low_r[f], above)
                left = jnp.where(first_lane, 0.0, pltpu.roll(low_t[f], 1, 1))
                right = jnp.where(last_lane, 0.0, pltpu.roll(high_t[f], LANES - 1, 1))
                value = (below + above) + (left + right)
                if mixing[f] != 0.0:
                    value = value + centre * u[f]
                slope[k, f] = value
                x_low[k + 1, f] = low_p[f]
                x_high[k + 1, f] = high_p[f]
            return carry

        lax.fori_loop(0, cells, row, 0, unroll=2)

    def halos(s):
        half_t, mix_t, half_p, mix_p, centre = [geo[i] for i in range(5)]
        phi_down, phi_up = phi_copies(s)
        theta_down, theta_up = theta_copies(s)

        def beside(side):
            u = [phi_in[s, side, f] for f in range(FIELDS)]
            speed, pressure = point_values(u)
            low, high = low_high(u, flux_of(u, speed, pressure, 2, {}, {}), half_p, mix_p)
            for f in range(FIELDS):
                if side == 0:
                    x_low[0, f] = low[f]
                else:
                    x_high[cells + 1, f] = high[f]

        @pl.when(a > 0)
        def _():
            phi_up.wait_recv()
            beside(0)

        @pl.when(a == 0)
        def _():
            for f in range(FIELDS):
                x_low[0, f] = wall[f] * x_high[1, f]

        @pl.when(a < n_ang - 1)
        def _():
            phi_down.wait_recv()
            beside(1)

        @pl.when(a == n_ang - 1)
        def _():
            for f in range(FIELDS):
                x_high[cells + 1, f] = wall[f] * x_low[cells, f]

        @pl.when(t > 0)
        def _():
            theta_up.wait_recv()

        @pl.when(t < n_rad - 1)
        def _():
            theta_down.wait_recv()

        @pl.when(at_low | at_high)
        def _():
            pltpu.make_async_copy(over_in.at[s], over_in.at[s], over_recv.at[s]).wait()
            ghost = jnp.sum(over_in[s], axis=0)
            nexts = pltpu.roll(ghost, LANES - side_rows, 1)
            lasts = pltpu.roll(ghost, side_rows, 1)
            is_theta = (block_of == 2) | (block_of == 5)
            is_phi = (block_of == 3) | (block_of == 6)
            ghost = jnp.where(
                is_theta, cosine * ghost + sine * nexts,
                jnp.where(is_phi, cosine * ghost - sine * lasts, ghost),
            )

            @pl.when(at_low)
            def _():
                theta_in[s, 0] = ghost

            @pl.when(at_high)
            def _():
                theta_in[s, 1] = ghost

        lower, upper = theta_in[s, 0], theta_in[s, 1]
        half_lane = LANES // 2
        is_low = lane8 < half_lane
        u = []
        for f in range(FIELDS):
            here = pltpu.roll(lower, LANES - f * cells, 1) if f else lower
            there = pltpu.roll(upper, (half_lane - f * cells) % LANES, 1)
            u.append(jnp.where(is_low, here, there))
        speed, pressure = point_values(u)
        signed = jnp.where(is_low, half_t, -half_t)
        edge, _ = low_high(u, flux_of(u, speed, pressure, 1, {}, {}), signed, mix_t)
        return edge

    def tend(k, f, edge):
        low = pltpu.roll(edge[f], lax.rem(LANES - k, LANES), 1)
        high = pltpu.roll(edge[f], LANES // 2 - 1 - k, 1)
        ends = jnp.where(first_lane, low, jnp.where(last_lane, high, 0.0))
        return (slope[k, f] + ends) + (x_low[k, f] + x_high[k + 2, f])

    zero8 = jnp.zeros((LEVELS, LANES), jnp.float32)

    def enter(k, packs):
        for f in range(FIELDS):
            value = land[f, pl.ds(k, LEVELS, stride=cells), :]
            state[0, k, f] = value
            packs = pack(k, f, value, packs)
        return packs

    packs = lax.fori_loop(0, cells, enter, (zero8, zero8), unroll=True)

    for s in range(4):
        send_all(s, packs)
        inner(s)
        edge = halos(s)
        if s < 3:
            def advance(k, packs):
                for f in range(FIELDS):
                    base = state[0, k, f]
                    k_now = tend(k, f, edge)
                    value = base + ahead[s] * k_now
                    state[s + 1, k, f] = value
                    packs = pack(k, f, value, packs)
                    total[k, f] = (base if s == 0 else total[k, f]) + share[s] * k_now
                return packs

            packs = lax.fori_loop(0, cells, advance, (zero8, zero8), unroll=True)
        else:
            def finish(k, carry):
                for f in range(FIELDS):
                    value = total[k, f] + share[s] * tend(k, f, edge)
                    staged[f, pl.ds(k, LEVELS, stride=cells), :] = value
                return carry

            lax.fori_loop(0, cells, finish, 0, unroll=True)

    gives = []
    for step in range(1, n_rad):
        to = lax.rem(t + step, n_rad)
        there = pl.ds(pl.multiple_of(to * rows, rows), rows)
        for i, (src, dst) in enumerate((
            (staged.at[0, there, :], oden.at[:, own_lanes]),
            (staged.at[pl.ds(1, 3), there, :], omom.at[:, :, own_lanes]),
            (staged.at[pl.ds(4, 3), there, :], omag.at[:, :, own_lanes]),
        )):
            gives.append(pltpu.make_async_remote_copy(
                src_ref=src, dst_ref=dst,
                send_sem=give_send.at[i, step], recv_sem=give_recv.at[i, step],
                device_id=at(mine, a, to), device_id_type=pl.DeviceIdType.MESH,
            ))
    for copy in gives:
        copy.start()
    keeps = [
        pltpu.make_async_copy(staged.at[0, own_rows, :], oden.at[:, own_lanes], own_sem.at[0]),
        pltpu.make_async_copy(staged.at[pl.ds(1, 3), own_rows, :], omom.at[:, :, own_lanes], own_sem.at[1]),
        pltpu.make_async_copy(staged.at[pl.ds(4, 3), own_rows, :], omag.at[:, :, own_lanes], own_sem.at[2]),
    ]
    for copy in keeps:
        copy.start()

    for copy in loads:
        copy.wait_send()
    pltpu.make_async_copy(meta_in, meta_in, meta_send).wait()
    for s in range(4):
        phi_down, phi_up = phi_copies(s)
        theta_down, theta_up = theta_copies(s)
        for can, copy in (
            (t > 0, theta_down), (t < n_rad - 1, theta_up),
            (a > 0, phi_down), (a < n_ang - 1, phi_up),
        ):
            pl.when(can)(copy.wait_send)
        pltpu.make_async_copy(over_out.at[s], over_out.at[s], over_send.at[s]).wait()
    for copy in keeps:
        copy.wait()
    for copy in gives:
        copy.wait()


def body(density, momentum, magnetic, partner_device, partner_phi, partner_theta, partner_weight,
         border_turn):
    _, rows_r, cells, n_theta = density.shape
    border = partner_phi.shape[1]
    n_ang, n_rad = lax.axis_size("ang"), lax.axis_size("rad")
    rows = rows_r * cells
    assert rows_r * n_rad == LEVELS and n_theta == LANES * n_rad and n_rad > 1
    assert LANES % border == 0 and n_ang % (LANES // border) == 0 and border == 2 * cells
    f32 = jnp.float32
    tiles = n_ang * border // LANES
    sources = n_ang * n_rad
    vmem = pltpu.VMEM
    dma = pltpu.SemaphoreType.DMA
    spaces = [pl.BlockSpec(memory_space=pl.ANY)] * 3 + [pl.BlockSpec(memory_space=vmem)] * 5
    outs = pl.pallas_call(
        functools.partial(kernel, (n_ang, n_rad, rows, cells, border)),
        out_shape=(
            jax.ShapeDtypeStruct((rows, n_theta), f32),
            jax.ShapeDtypeStruct((3, rows, n_theta), f32),
            jax.ShapeDtypeStruct((3, rows, n_theta), f32),
        ),
        in_specs=spaces,
        out_specs=[pl.BlockSpec(memory_space=pl.ANY)] * 3,
        scratch_shapes=[
            vmem((FIELDS, LEVELS * cells, LANES), f32),
            vmem((FIELDS, LEVELS * cells, LANES), f32),
            vmem((4, cells, FIELDS, LEVELS, LANES), f32),
            vmem((cells, FIELDS, LEVELS, LANES), f32),
            vmem((cells, FIELDS, LEVELS, LANES), f32),
            vmem((cells + 2, FIELDS, LEVELS, LANES), f32),
            vmem((cells + 2, FIELDS, LEVELS, LANES), f32),
            vmem((5, LEVELS, LANES), f32),
            vmem((4, 2, FIELDS, LEVELS, LANES), f32),
            vmem((4, 2, LEVELS, LANES), f32),
            vmem((4, 2, LEVELS, LANES), f32),
            vmem((4, 2 * n_ang, LEVELS, LANES), f32),
            vmem((4, sources, LEVELS, LANES), f32),
            vmem((LEVELS, LANES), f32),
            vmem((n_ang, LEVELS, LANES), f32),
            vmem((tiles, 2, cells, LANES), f32),
            vmem((tiles, 2 * LANES, 2 * LANES), jnp.bfloat16),
            dma((3,)), dma((3, n_rad)), dma((3, n_rad)), dma((3, n_rad)), dma((3, n_rad)),
            dma, dma, dma((4, 2)), dma((4, 2)), dma((4, 2)), dma((4, 2)), dma((4,)), dma((4,)),
        ],
        compiler_params=pltpu.CompilerParams(
            collective_id=0, has_side_effects=True, vmem_limit_bytes=32 * 1024 * 1024
        ),
    )(
        density.reshape(rows, n_theta),
        momentum.reshape(3, rows, n_theta),
        magnetic.reshape(3, rows, n_theta),
        partner_device.reshape(border, 1),
        partner_phi, partner_theta,
        partner_weight.reshape(border, 4),
        border_turn,
    )
    return (
        outs[0].reshape(density.shape),
        outs[1].reshape(momentum.shape),
        outs[2].reshape(magnetic.shape),
    )


def solution(mesh):
    in_specs = (
        P("panel", "rad", "ang", None),
        P("panel", None, "rad", "ang", None),
        P("panel", None, "rad", "ang", None),
        P("panel", "ang", None),
        P("panel", "ang"),
        P("panel", "ang"),
        P("panel", "ang", None),
        P("panel", "ang"),
    )
    out_specs = (
        P("panel", "rad", "ang", None),
        P("panel", None, "rad", "ang", None),
        P("panel", None, "rad", "ang", None),
    )
    return jax.shard_map(body, mesh=mesh, in_specs=in_specs, out_specs=out_specs, check_vma=False)
```

```python
import functools
import math

import jax
import jax.numpy as jnp
from jax import lax
from jax.experimental import pallas as pl
from jax.experimental.pallas import tpu as pltpu
from jax.sharding import PartitionSpec as P

time_step = 0.15
mixing = (0.0, 0.1, 0.1, 0.1, 0.1, 0.1, 0.1)
wall = (1.0, -1.0, -1.0, -1.0, 1.0, 1.0, 1.0)
r_inner = 0.35
FIELDS = 7
LANES = 128
LEVELS = 8
vmem_bytes = 64 * 1024 * 1024 - 256 * 1024
ahead = (0.5 * time_step, 0.5 * time_step, time_step)
share = (time_step / 6.0, time_step / 3.0, time_step / 3.0, time_step / 6.0)


def point_values(u):
    rate = 1.0 / u[0]
    speed = [u[1 + c] * rate for c in range(3)]
    pressure = u[0] + 0.5 * (u[4] * u[4] + u[5] * u[5] + u[6] * u[6])
    return speed, pressure


def flux_of(u, speed, pressure, d, stress, twist):
    out = [u[1 + d]]
    for c in range(3):
        key = (min(c, d), max(c, d))
        if key not in stress:
            term = u[1 + c] * speed[d] - u[4 + c] * u[4 + d]
            stress[key] = term + pressure if c == d else term
        out.append(stress[key])
    for c in range(3):
        if c == d:
            out.append(None)
            continue
        key = (min(c, d), max(c, d))
        if key not in twist:
            low, high = key
            twist[key] = speed[high] * u[4 + low] - u[4 + high] * speed[low]
        out.append(twist[key] if c == key[0] else -twist[key])
    return out


def low_high(u, flux, half, mix):
    low, high = [], []
    for f in range(FIELDS):
        carried = None if flux[f] is None else half * flux[f]
        spread = None if mixing[f] == 0.0 else mix * u[f]
        if carried is None:
            low.append(spread)
            high.append(spread)
        elif spread is None:
            low.append(carried)
            high.append(-carried)
        else:
            low.append(spread + carried)
            high.append(spread - carried)
    return low, high


def kernel(
    sizes,
    den, mom, mag, pdev_hbm, pphi_hbm, ptheta_hbm, pweight_hbm, pturn_hbm,
    oden, omom, omag,
    pdev, pphi, ptheta, pweight, pturn,
    land, staged, state, total, slope, x_low, x_high, geo,
    phi_in, theta_out, theta_in, over_out, over_in,
    meta_out, meta_in, coef, picker,
    small_sem, own_sem, load_send, load_recv, give_send, give_recv,
    meta_send, meta_recv, phi_send, phi_recv, theta_send, theta_recv,
    over_send, over_recv,
):
    n_ang, n_rad, rows, cells, border = sizes
    side_rows = border // 2
    per_tile = LANES // border
    tiles = n_ang // per_tile
    sources = n_ang * n_rad
    mine = lax.axis_index("panel")
    a = lax.axis_index("ang")
    t = lax.axis_index("rad")
    other = 1 - mine

    def at(panel, ang, rad):
        return {"panel": panel, "ang": ang, "rad": rad}

    small = [
        pltpu.make_async_copy(src, dst, small_sem.at[i])
        for i, (src, dst) in enumerate((
            (pdev_hbm, pdev), (pphi_hbm, pphi), (ptheta_hbm, ptheta),
            (pweight_hbm, pweight), (pturn_hbm, pturn),
        ))
    ]
    for copy in small:
        copy.start()

    barrier = pltpu.get_barrier_semaphore()

    def greet(i, carry):
        pl.semaphore_signal(
            barrier, inc=1,
            device_id=at(other, i // n_rad, lax.rem(i, n_rad)),
            device_id_type=pl.DeviceIdType.MESH,
        )
        return carry

    lax.fori_loop(0, sources, greet, 0)
    for step in range(1, n_rad):
        pl.semaphore_signal(
            barrier, inc=1, device_id=at(mine, a, lax.rem(t + step, n_rad)),
            device_id_type=pl.DeviceIdType.MESH,
        )

    @pl.when(a > 0)
    def _():
        pl.semaphore_signal(
            barrier, inc=1, device_id=at(mine, a - 1, t), device_id_type=pl.DeviceIdType.MESH
        )

    @pl.when(a < n_ang - 1)
    def _():
        pl.semaphore_signal(
            barrier, inc=1, device_id=at(mine, a + 1, t), device_id_type=pl.DeviceIdType.MESH
        )

    own_rows = pl.ds(pl.multiple_of(t * rows, rows), rows)
    own_lanes = pl.ds(pl.multiple_of(t * LANES, LANES), LANES)
    own = [
        pltpu.make_async_copy(den.at[:, own_lanes], land.at[0, own_rows, :], own_sem.at[0]),
        pltpu.make_async_copy(mom.at[:, :, own_lanes], land.at[pl.ds(1, 3), own_rows, :], own_sem.at[1]),
        pltpu.make_async_copy(mag.at[:, :, own_lanes], land.at[pl.ds(4, 3), own_rows, :], own_sem.at[2]),
    ]
    for copy in own:
        copy.start()

    sub8 = lax.broadcasted_iota(jnp.int32, (LEVELS, LANES), 0)
    lane8 = lax.broadcasted_iota(jnp.int32, (LEVELS, LANES), 1)
    sub_b = lax.broadcasted_iota(jnp.int32, (border, LANES), 0)
    lane_b = lax.broadcasted_iota(jnp.int32, (border, LANES), 1)
    square = (
        lax.broadcasted_iota(jnp.int32, (border, border), 0)
        == lax.broadcasted_iota(jnp.int32, (border, border), 1)
    )

    def column(row):
        wide = jnp.broadcast_to(row, (border, border))
        return jnp.sum(jnp.where(square, wide, 0.0), axis=1, keepdims=True)

    spot_b = jnp.where(sub_b < side_rows, 2 * sub_b, 2 * sub_b - (border - 1))
    place = lane_b == spot_b + border * lax.rem(a, per_tile)
    for copy in small:
        copy.wait()
    columns = [
        column(pdev[...].astype(jnp.float32)),
        column(pphi[...].astype(jnp.float32)),
        column(ptheta[...].astype(jnp.float32)),
    ] + [column(pweight[i:i + 1, :]) for i in range(4)]
    meta_out[...] = jnp.zeros_like(meta_out)
    for i, col in enumerate(columns):
        meta_out[i:i + 1, :] = jnp.sum(
            jnp.where(place, jnp.broadcast_to(col, (border, LANES)), 0.0), axis=0, keepdims=True
        )

    at_low = t == 0
    at_high = t == n_rad - 1
    shifted = jnp.where(spot_b % 2 == 0, spot_b, lax.rem(spot_b + LANES - 2, LANES))
    ghosted = jnp.where(shifted % 2 == 0, at_low.astype(jnp.int32), at_high.astype(jnp.int32))
    turn_at = (lane_b == shifted) & (ghosted == 1)
    angle = jnp.sum(
        jnp.where(turn_at, jnp.broadcast_to(column(pturn[...]), (border, LANES)), 0.0),
        axis=0, keepdims=True,
    )
    angle = jnp.broadcast_to(angle, (LEVELS, LANES))
    cosine, sine = jnp.cos(angle), jnp.sin(angle)

    radius = r_inner + (sub8.astype(jnp.float32) + 0.5) * ((1.0 - r_inner) / LEVELS)
    theta = math.pi / 4 + ((lane8 + t * LANES).astype(jnp.float32) + 0.5) * (
        math.pi / 2 / (LANES * n_rad)
    )
    inv_radius = 1.0 / radius
    inv_both = inv_radius / jnp.sin(theta)
    half_t = 0.5 * inv_radius
    mix_t = 0.1 * inv_radius * inv_radius
    half_p = 0.5 * inv_both
    mix_p = 0.1 * inv_both * inv_both
    centre = -2.0 * (0.1 + mix_t + mix_p)
    for i, value in enumerate((half_t, mix_t, half_p, mix_p, centre)):
        geo[i] = value

    pl.semaphore_wait(
        barrier,
        sources + n_rad - 1 + jnp.where(a > 0, 1, 0) + jnp.where(a < n_ang - 1, 1, 0),
    )

    loads = []
    for step in range(1, n_rad):
        to = lax.rem(t + step, n_rad)
        lanes = pl.ds(pl.multiple_of(to * LANES, LANES), LANES)
        for i, (src, dst) in enumerate((
            (den.at[:, lanes], land.at[0, own_rows, :]),
            (mom.at[:, :, lanes], land.at[pl.ds(1, 3), own_rows, :]),
            (mag.at[:, :, lanes], land.at[pl.ds(4, 3), own_rows, :]),
        )):
            loads.append(pltpu.make_async_remote_copy(
                src_ref=src, dst_ref=dst,
                send_sem=load_send.at[i, step], recv_sem=load_recv.at[i, step],
                device_id=at(mine, a, to), device_id_type=pl.DeviceIdType.MESH,
            ))
    for copy in loads:
        copy.start()

    def meta_copy(to):
        return pltpu.make_async_remote_copy(
            src_ref=meta_out, dst_ref=meta_in.at[a],
            send_sem=meta_send, recv_sem=meta_recv,
            device_id=at(other, to, t), device_id_type=pl.DeviceIdType.MESH,
        )

    def send_meta(to, carry):
        meta_copy(to).start()
        return carry

    lax.fori_loop(0, n_ang, send_meta, 0)
    pltpu.make_async_copy(meta_in, meta_in, meta_recv).wait()

    sub_l = lax.broadcasted_iota(jnp.int32, (LANES, LANES), 0)
    sub_c = lax.broadcasted_iota(jnp.int32, (cells, LANES), 0)

    def prepare(g, carry):
        table = jnp.sum(meta_in[pl.ds(g * per_tile, per_tile)], axis=0)
        device = table[0:1].astype(jnp.int32)
        at_phi = table[1:2].astype(jnp.int32)
        at_theta = table[2:3].astype(jnp.int32) - t * LANES
        hit = jnp.broadcast_to(device == a, (cells, LANES))
        near = hit & (sub_c == at_phi)
        far = hit & (sub_c == at_phi + 1)
        zero = jnp.zeros((cells, LANES), jnp.float32)
        w = [jnp.broadcast_to(table[3 + i:4 + i], (cells, LANES)) for i in range(4)]
        coef[g, 0] = jnp.where(near, w[0], jnp.where(far, w[2], zero))
        coef[g, 1] = jnp.where(near, w[1], jnp.where(far, w[3], zero))
        first = jnp.where(sub_l == at_theta, 1.0, 0.0).astype(jnp.bfloat16)
        second = jnp.where(sub_l == at_theta + 1, 1.0, 0.0).astype(jnp.bfloat16)
        for part in range(2):
            picker[g, pl.ds(part * LANES, LANES), pl.ds(0, LANES)] = first
            picker[g, pl.ds(part * LANES, LANES), pl.ds(LANES, LANES)] = second
        return carry

    if tiles == 1:
        prepare(0, 0)
    else:
        lax.fori_loop(0, tiles, prepare, 0)

    for copy in own:
        copy.wait()
    for copy in loads:
        copy.wait_recv()

    block_of = lane8 // border
    pair8 = lane8 // 2
    even = lane8 % 2 == 0
    first_lane = lane8 == 0
    last_lane = lane8 == LANES - 1
    first_level = sub8 == 0
    last_level = sub8 == LEVELS - 1

    def pack(k, f, value, packs):
        spot = border * (f % per_tile) + 2 * k + 1
        hit = pair8 == border // 2 * (f % per_tile) + k
        packs[f // per_tile] = jnp.where(
            hit, pltpu.roll(value, lax.rem(spot, LANES), 1), packs[f // per_tile]
        )

    def phi_copies(s):
        down = pltpu.make_async_remote_copy(
            src_ref=state.at[s, 0], dst_ref=phi_in.at[s, 1],
            send_sem=phi_send.at[s, 0], recv_sem=phi_recv.at[s, 1],
            device_id=at(mine, a, t) | {"ang": jnp.maximum(a - 1, 0)},
            device_id_type=pl.DeviceIdType.MESH,
        )
        up = pltpu.make_async_remote_copy(
            src_ref=state.at[s, cells - 1], dst_ref=phi_in.at[s, 0],
            send_sem=phi_send.at[s, 1], recv_sem=phi_recv.at[s, 0],
            device_id=at(mine, a, t) | {"ang": jnp.minimum(a + 1, n_ang - 1)},
            device_id_type=pl.DeviceIdType.MESH,
        )
        return down, up

    def theta_copies(s):
        down = pltpu.make_async_remote_copy(
            src_ref=theta_out.at[s], dst_ref=theta_in.at[s, 1],
            send_sem=theta_send.at[s, 0], recv_sem=theta_recv.at[s, 1],
            device_id=at(mine, a, jnp.maximum(t - 1, 0)),
            device_id_type=pl.DeviceIdType.MESH,
        )
        up = pltpu.make_async_remote_copy(
            src_ref=theta_out.at[s], dst_ref=theta_in.at[s, 0],
            send_sem=theta_send.at[s, 1], recv_sem=theta_recv.at[s, 0],
            device_id=at(mine, a, jnp.minimum(t + 1, n_rad - 1)),
            device_id_type=pl.DeviceIdType.MESH,
        )
        return down, up

    def over_copy(s, q):
        return pltpu.make_async_remote_copy(
            src_ref=over_out.at[s, q // 2], dst_ref=over_in.at[s, a * n_rad + t],
            send_sem=over_send.at[s], recv_sem=over_recv.at[s],
            device_id=at(other, q // 2, lax.rem(q, 2) * (n_rad - 1)),
            device_id_type=pl.DeviceIdType.MESH,
        )

    def send_all(s):
        theta_down, theta_up = theta_copies(s)
        phi_down, phi_up = phi_copies(s)
        for can, copy in (
            (t > 0, theta_down), (t < n_rad - 1, theta_up),
            (a > 0, phi_down), (a < n_ang - 1, phi_up),
        ):
            pl.when(can)(copy.start)

        def overset(g, carry):
            value = state[s].reshape(cells * FIELDS * LEVELS, LANES)
            head = value.astype(jnp.bfloat16)
            rest = (value - head.astype(jnp.float32)).astype(jnp.bfloat16)
            got = jnp.dot(
                jnp.concatenate([head, rest], axis=1), picker[g],
                preferred_element_type=jnp.float32,
            )
            ghosts = [None] * FIELDS
            for k in range(cells):
                near = jnp.broadcast_to(coef[g, 0, k:k + 1, :], (LEVELS, LANES))
                far = jnp.broadcast_to(coef[g, 1, k:k + 1, :], (LEVELS, LANES))
                for f in range(FIELDS):
                    at_row = (k * FIELDS + f) * LEVELS
                    piece = got[at_row:at_row + LEVELS]
                    term = piece[:, :LANES] * near + piece[:, LANES:] * far
                    ghosts[f] = term if k == 0 else ghosts[f] + term
            turned = [
                pltpu.roll(ghosts[f], border * (f % per_tile), 1) if f % per_tile else ghosts[f]
                for f in range(FIELDS)
            ]
            for j in range(per_tile):
                for half in range(2):
                    members = range(half * per_tile, min(FIELDS, (half + 1) * per_tile))
                    message = turned[members[0]]
                    for f in members:
                        message = jnp.where(
                            block_of == (f + j) % per_tile, turned[f], message
                        )
                    if j:
                        message = pltpu.roll(message, LANES - j * border, 1)
                    over_out[s, g * per_tile + j, half] = message
            for j in range(2 * per_tile):
                over_copy(s, g * 2 * per_tile + j).start()
            return carry

        if tiles == 1:
            overset(0, 0)
        else:
            lax.fori_loop(0, tiles, overset, 0)

    def inner(s):
        half_t, mix_t, half_p, mix_p, centre = [geo[i] for i in range(5)]

        def row(k, carry):
            u = [state[s, k, f] for f in range(FIELDS)]
            speed, pressure = point_values(u)
            stress, twist = {}, {}
            low_r, high_r = low_high(u, flux_of(u, speed, pressure, 0, stress, twist), 0.5, 0.1)
            low_t, high_t = low_high(u, flux_of(u, speed, pressure, 1, stress, twist), half_t, mix_t)
            low_p, high_p = low_high(u, flux_of(u, speed, pressure, 2, stress, twist), half_p, mix_p)
            for f in range(FIELDS):
                below = pltpu.roll(low_r[f], 1, 0)
                above = pltpu.roll(high_r[f], LEVELS - 1, 0)
                below = jnp.where(first_level, wall[f] * high_r[f], below)
                above = jnp.where(last_level, wall[f] * low_r[f], above)
                left = jnp.where(first_lane, 0.0, pltpu.roll(low_t[f], 1, 1))
                right = jnp.where(last_lane, 0.0, pltpu.roll(high_t[f], LANES - 1, 1))
                value = (below + above) + (left + right)
                if mixing[f] != 0.0:
                    value = value + centre * u[f]
                slope[k, f] = value
                x_low[k + 1, f] = low_p[f]
                x_high[k + 1, f] = high_p[f]
            return carry

        lax.fori_loop(0, cells, row, 0, unroll=4)

    def halos(s):
        half_t, mix_t, half_p, mix_p, centre = [geo[i] for i in range(5)]
        phi_down, phi_up = phi_copies(s)
        theta_down, theta_up = theta_copies(s)

        def beside(side):
            u = [phi_in[s, side, f] for f in range(FIELDS)]
            speed, pressure = point_values(u)
            low, high = low_high(u, flux_of(u, speed, pressure, 2, {}, {}), half_p, mix_p)
            for f in range(FIELDS):
                if side == 0:
                    x_low[0, f] = low[f]
                else:
                    x_high[cells + 1, f] = high[f]

        @pl.when(a > 0)
        def _():
            phi_up.wait_recv()
            beside(0)

        @pl.when(a == 0)
        def _():
            for f in range(FIELDS):
                x_low[0, f] = wall[f] * x_high[1, f]

        @pl.when(a < n_ang - 1)
        def _():
            phi_down.wait_recv()
            beside(1)

        @pl.when(a == n_ang - 1)
        def _():
            for f in range(FIELDS):
                x_high[cells + 1, f] = wall[f] * x_low[cells, f]

        @pl.when(t > 0)
        def _():
            theta_up.wait_recv()

        @pl.when(t < n_rad - 1)
        def _():
            theta_down.wait_recv()

        @pl.when(at_low | at_high)
        def _():
            pltpu.make_async_copy(over_in.at[s], over_in.at[s], over_recv.at[s]).wait()
            ghost = jnp.sum(over_in[s], axis=0)
            @pl.when(at_low)
            def _():
                theta_in[s, 0] = ghost

            @pl.when(at_high)
            def _():
                theta_in[s, 1] = ghost

        both = [
            jnp.where(even, theta_in[s, 0, h], pltpu.roll(theta_in[s, 1, h], LANES - 2, 1))
            for h in range(2)
        ]
        u = []
        for f in range(FIELDS):
            away = border * (f % per_tile)
            value = both[f // per_tile]
            u.append(pltpu.roll(value, LANES - away, 1) if away else value)
        for f in (2, 5):
            u[f], u[f + 1] = cosine * u[f] + sine * u[f + 1], cosine * u[f + 1] - sine * u[f]
        speed, pressure = point_values(u)
        signed = jnp.where(even, half_t, -half_t)
        edge, _ = low_high(u, flux_of(u, speed, pressure, 1, {}, {}), signed, mix_t)
        return edge

    def tend(k, f, edge):
        ends = pltpu.roll(edge[f], lax.rem(LANES - 2 * k, LANES), 1)
        ends = jnp.where(outer_lanes, ends, 0.0)
        return (slope[k, f] + ends) + (x_low[k, f] + x_high[k + 2, f])

    zero8 = jnp.zeros((LEVELS, LANES), jnp.float32)
    outer_lanes = first_lane | last_lane

    def enter(k, packs):
        packs = list(packs)
        for f in range(FIELDS):
            value = land[f, pl.ds(k, LEVELS, stride=cells), :]
            state[0, k, f] = value
            total[k, f] = value
            pack(k, f, value, packs)
        return tuple(packs)

    def keep(s, packs):
        for half in range(2):
            theta_out[s, half] = packs[half]

    keep(0, lax.fori_loop(0, cells, enter, (zero8, zero8), unroll=4))

    def stage(s, carry):
        send_all(s)
        inner(s)
        edge = halos(s)
        step_on = jnp.where(s < 2, ahead[0], ahead[2])
        weight = jnp.where((s == 0) | (s == 3), share[0], share[1])

        def advance(k, packs):
            packs = list(packs)
            for f in range(FIELDS):
                now = tend(k, f, edge)
                value = state[0, k, f] + step_on * now
                state[s + 1, k, f] = value
                pack(k, f, value, packs)
                total[k, f] = total[k, f] + weight * now
            return tuple(packs)

        keep(s + 1, lax.fori_loop(0, cells, advance, (zero8, zero8), unroll=4))
        return carry

    lax.fori_loop(0, 4, stage, 0)

    def leave(k, carry):
        for f in range(FIELDS):
            staged[f, pl.ds(k, LEVELS, stride=cells), :] = total[k, f]
        return carry

    lax.fori_loop(0, cells, leave, 0, unroll=4)

    gives = []
    for step in range(1, n_rad):
        to = lax.rem(t + step, n_rad)
        there = pl.ds(pl.multiple_of(to * rows, rows), rows)
        for i, (src, dst) in enumerate((
            (staged.at[0, there, :], oden.at[:, own_lanes]),
            (staged.at[pl.ds(1, 3), there, :], omom.at[:, :, own_lanes]),
            (staged.at[pl.ds(4, 3), there, :], omag.at[:, :, own_lanes]),
        )):
            gives.append(pltpu.make_async_remote_copy(
                src_ref=src, dst_ref=dst,
                send_sem=give_send.at[i, step], recv_sem=give_recv.at[i, step],
                device_id=at(mine, a, to), device_id_type=pl.DeviceIdType.MESH,
            ))
    for copy in gives:
        copy.start()
    keeps = [
        pltpu.make_async_copy(staged.at[0, own_rows, :], oden.at[:, own_lanes], own_sem.at[0]),
        pltpu.make_async_copy(staged.at[pl.ds(1, 3), own_rows, :], omom.at[:, :, own_lanes], own_sem.at[1]),
        pltpu.make_async_copy(staged.at[pl.ds(4, 3), own_rows, :], omag.at[:, :, own_lanes], own_sem.at[2]),
    ]
    for copy in keeps:
        copy.start()

    for copy in loads:
        copy.wait_send()
    pltpu.make_async_copy(meta_in, meta_in, meta_send).wait()
    for s in range(4):
        phi_down, phi_up = phi_copies(s)
        theta_down, theta_up = theta_copies(s)
        for can, copy in (
            (t > 0, theta_down), (t < n_rad - 1, theta_up),
            (a > 0, phi_down), (a < n_ang - 1, phi_up),
        ):
            pl.when(can)(copy.wait_send)
        for _ in range(2):
            pltpu.make_async_copy(over_out.at[s], over_out.at[s], over_send.at[s]).wait()
    for copy in keeps:
        copy.wait()
    for copy in gives:
        copy.wait()


def hand_over(one, two, three, out_one, out_two, out_three, sems):
    copies = [
        pltpu.make_async_copy(src, dst, sems.at[i])
        for i, (src, dst) in enumerate(
            [(one, out_one)]
            + [(two.at[c], out_two.at[c]) for c in range(3)]
            + [(three.at[c], out_three.at[c]) for c in range(3)]
        )
    ]
    for copy in copies:
        copy.start()
    for copy in copies:
        copy.wait()


def body(density, momentum, magnetic, partner_device, partner_phi, partner_theta, partner_weight,
         border_turn):
    _, rows_r, cells, n_theta = density.shape
    border = partner_phi.shape[1]
    n_ang, n_rad = lax.axis_size("ang"), lax.axis_size("rad")
    rows = rows_r * cells
    assert rows_r * n_rad == LEVELS and n_theta == LANES * n_rad and n_rad > 1
    assert border * 4 == LANES and n_ang % (LANES // border) == 0 and border == 2 * cells
    f32 = jnp.float32
    tiles = n_ang * border // LANES
    sources = n_ang * n_rad
    vmem = pltpu.VMEM
    dma = pltpu.SemaphoreType.DMA
    spaces = [pl.BlockSpec(memory_space=pltpu.HBM)] * 8
    outs = pl.pallas_call(
        functools.partial(kernel, (n_ang, n_rad, rows, cells, border)),
        out_shape=(
            jax.ShapeDtypeStruct((rows, n_theta), f32),
            jax.ShapeDtypeStruct((3, rows, n_theta), f32),
            jax.ShapeDtypeStruct((3, rows, n_theta), f32),
        ),
        in_specs=spaces,
        out_specs=[pl.BlockSpec(memory_space=pl.ANY)] * 3,
        scratch_shapes=[
            vmem((1, border), jnp.int32), vmem((1, border), jnp.int32),
            vmem((1, border), jnp.int32), vmem((4, border), f32), vmem((1, border), f32),
            vmem((FIELDS, LEVELS * cells, LANES), f32),
            vmem((FIELDS, LEVELS * cells, LANES), f32),
            vmem((5, cells, FIELDS, LEVELS, LANES), f32),
            vmem((cells, FIELDS, LEVELS, LANES), f32),
            vmem((cells, FIELDS, LEVELS, LANES), f32),
            vmem((cells + 2, FIELDS, LEVELS, LANES), f32),
            vmem((cells + 2, FIELDS, LEVELS, LANES), f32),
            vmem((5, LEVELS, LANES), f32),
            vmem((4, 2, FIELDS, LEVELS, LANES), f32),
            vmem((5, 2, LEVELS, LANES), f32),
            vmem((4, 2, 2, LEVELS, LANES), f32),
            vmem((4, n_ang, 2, LEVELS, LANES), f32),
            vmem((4, sources, 2, LEVELS, LANES), f32),
            vmem((LEVELS, LANES), f32),
            vmem((n_ang, LEVELS, LANES), f32),
            vmem((tiles, 2, cells, LANES), f32),
            vmem((tiles, 2 * LANES, 2 * LANES), jnp.bfloat16),
            dma((5,)), dma((3,)), dma((3, n_rad)), dma((3, n_rad)), dma((3, n_rad)), dma((3, n_rad)),
            dma, dma, dma((4, 2)), dma((4, 2)), dma((4, 2)), dma((4, 2)), dma((4,)), dma((4,)),
        ],
        compiler_params=pltpu.CompilerParams(
            collective_id=0, has_side_effects=True, vmem_limit_bytes=vmem_bytes
        ),
    )(
        density.reshape(rows, n_theta),
        momentum.reshape(3, rows, n_theta),
        magnetic.reshape(3, rows, n_theta),
        partner_device.reshape(1, border),
        partner_phi, partner_theta,
        partner_weight.reshape(border, 4).T,
        border_turn,
    )
    outs = pl.pallas_call(
        hand_over,
        out_shape=tuple(jax.ShapeDtypeStruct(o.shape, f32) for o in outs),
        in_specs=[pl.BlockSpec(memory_space=pl.ANY)] * 3,
        out_specs=[pl.BlockSpec(memory_space=pltpu.HBM)] * 3,
        scratch_shapes=[dma((FIELDS,))],
        compiler_params=pltpu.CompilerParams(vmem_limit_bytes=vmem_bytes),
    )(*outs)
    return (
        outs[0].reshape(density.shape),
        outs[1].reshape(momentum.shape),
        outs[2].reshape(magnetic.shape),
    )


def solution(mesh):
    in_specs = (
        P("panel", "rad", "ang", None),
        P("panel", None, "rad", "ang", None),
        P("panel", None, "rad", "ang", None),
        P("panel", "ang", None),
        P("panel", "ang"),
        P("panel", "ang"),
        P("panel", "ang", None),
        P("panel", "ang"),
    )
    out_specs = (
        P("panel", "rad", "ang", None),
        P("panel", None, "rad", "ang", None),
        P("panel", None, "rad", "ang", None),
    )
    return jax.shard_map(body, mesh=mesh, in_specs=in_specs, out_specs=out_specs, check_vma=False)
```

```python
import functools
import math

import jax
import jax.numpy as jnp
from jax import lax
from jax.experimental import pallas as pl
from jax.experimental.pallas import tpu as pltpu
from jax.sharding import PartitionSpec as P

time_step = 0.15
mixing = (0.0, 0.1, 0.1, 0.1, 0.1, 0.1, 0.1)
wall = (1.0, -1.0, -1.0, -1.0, 1.0, 1.0, 1.0)
r_inner = 0.35
FIELDS = 7
LANES = 128
LEVELS = 8
vmem_bytes = 32 * 1024 * 1024
ahead = (0.5 * time_step, 0.5 * time_step, time_step)
share = (time_step / 6.0, time_step / 3.0, time_step / 3.0, time_step / 6.0)


def point_values(u):
    rate = 1.0 / u[0]
    speed = [u[1 + c] * rate for c in range(3)]
    pressure = u[0] + 0.5 * (u[4] * u[4] + u[5] * u[5] + u[6] * u[6])
    return speed, pressure


def flux_of(u, speed, pressure, d, stress, twist):
    out = [u[1 + d]]
    for c in range(3):
        key = (min(c, d), max(c, d))
        if key not in stress:
            term = u[1 + c] * speed[d] - u[4 + c] * u[4 + d]
            stress[key] = term + pressure if c == d else term
        out.append(stress[key])
    for c in range(3):
        if c == d:
            out.append(None)
            continue
        key = (min(c, d), max(c, d))
        if key not in twist:
            low, high = key
            twist[key] = speed[high] * u[4 + low] - u[4 + high] * speed[low]
        out.append(twist[key] if c == key[0] else -twist[key])
    return out


def low_high(u, flux, half, mix):
    low, high = [], []
    for f in range(FIELDS):
        carried = None if flux[f] is None else half * flux[f]
        spread = None if mixing[f] == 0.0 else mix * u[f]
        if carried is None:
            low.append(spread)
            high.append(spread)
        elif spread is None:
            low.append(carried)
            high.append(-carried)
        else:
            low.append(spread + carried)
            high.append(spread - carried)
    return low, high


def kernel(
    sizes,
    den, mom, mag, pdev_hbm, pphi_hbm, ptheta_hbm, pweight_hbm, pturn_hbm,
    oden, omom, omag,
    pdev, pphi, ptheta, pweight, pturn, first, fetch_sem,
    land, staged, state, total, slope, x_low, x_high, geo,
    phi_in, theta_out, theta_in, over_out, over_in,
    meta_out, meta_in, coef, picker,
    small_sem, own_sem, load_send, load_recv, give_send, give_recv,
    meta_send, meta_recv, phi_send, phi_recv, theta_send, theta_recv,
    over_send, over_recv,
):
    n_ang, n_rad, rows, cells, border = sizes
    side_rows = border // 2
    per_tile = LANES // border
    tiles = n_ang // per_tile
    sources = n_ang * n_rad
    mine = lax.axis_index("panel")
    a = lax.axis_index("ang")
    t = lax.axis_index("rad")
    other = 1 - mine

    def at(panel, ang, rad):
        return {"panel": panel, "ang": ang, "rad": rad}

    small = [
        pltpu.make_async_copy(src, dst, small_sem.at[i])
        for i, (src, dst) in enumerate((
            (pdev_hbm, pdev), (pphi_hbm, pphi), (ptheta_hbm, ptheta),
            (pweight_hbm, pweight), (pturn_hbm, pturn),
        ))
    ]
    for copy in small:
        copy.start()
    fetches = [
        pltpu.make_async_copy(den, first.at[0], fetch_sem.at[0]),
        pltpu.make_async_copy(mom, first.at[pl.ds(1, 3)], fetch_sem.at[1]),
        pltpu.make_async_copy(mag, first.at[pl.ds(4, 3)], fetch_sem.at[2]),
    ]
    for copy in fetches:
        copy.start()

    barrier = pltpu.get_barrier_semaphore()

    def greet(i, carry):
        pl.semaphore_signal(
            barrier, inc=1,
            device_id=at(other, i // n_rad, lax.rem(i, n_rad)),
            device_id_type=pl.DeviceIdType.MESH,
        )
        return carry

    lax.fori_loop(0, sources, greet, 0)
    for step in range(1, n_rad):
        pl.semaphore_signal(
            barrier, inc=1, device_id=at(mine, a, lax.rem(t + step, n_rad)),
            device_id_type=pl.DeviceIdType.MESH,
        )

    @pl.when(a > 0)
    def _():
        pl.semaphore_signal(
            barrier, inc=1, device_id=at(mine, a - 1, t), device_id_type=pl.DeviceIdType.MESH
        )

    @pl.when(a < n_ang - 1)
    def _():
        pl.semaphore_signal(
            barrier, inc=1, device_id=at(mine, a + 1, t), device_id_type=pl.DeviceIdType.MESH
        )

    own_rows = pl.ds(pl.multiple_of(t * rows, rows), rows)
    own_lanes = pl.ds(pl.multiple_of(t * LANES, LANES), LANES)
    own = [
        pltpu.make_async_copy(den.at[:, own_lanes], land.at[0, own_rows, :], own_sem.at[0]),
        pltpu.make_async_copy(mom.at[:, :, own_lanes], land.at[pl.ds(1, 3), own_rows, :], own_sem.at[1]),
        pltpu.make_async_copy(mag.at[:, :, own_lanes], land.at[pl.ds(4, 3), own_rows, :], own_sem.at[2]),
    ]
    for copy in own:
        copy.start()

    sub8 = lax.broadcasted_iota(jnp.int32, (LEVELS, LANES), 0)
    lane8 = lax.broadcasted_iota(jnp.int32, (LEVELS, LANES), 1)
    sub_b = lax.broadcasted_iota(jnp.int32, (border, LANES), 0)
    lane_b = lax.broadcasted_iota(jnp.int32, (border, LANES), 1)
    square = (
        lax.broadcasted_iota(jnp.int32, (border, border), 0)
        == lax.broadcasted_iota(jnp.int32, (border, border), 1)
    )

    def column(row):
        wide = jnp.broadcast_to(row, (border, border))
        return jnp.sum(jnp.where(square, wide, 0.0), axis=1, keepdims=True)

    spot_b = jnp.where(sub_b < side_rows, 2 * sub_b, 2 * sub_b - (border - 1))
    place = lane_b == spot_b + border * lax.rem(a, per_tile)
    for copy in small:
        copy.wait()
    columns = [
        column(pdev[...].astype(jnp.float32)),
        column(pphi[...].astype(jnp.float32)),
        column(ptheta[...].astype(jnp.float32)),
    ] + [column(pweight[i:i + 1, :]) for i in range(4)]
    meta_out[...] = jnp.zeros_like(meta_out)
    for i, col in enumerate(columns):
        meta_out[i:i + 1, :] = jnp.sum(
            jnp.where(place, jnp.broadcast_to(col, (border, LANES)), 0.0), axis=0, keepdims=True
        )

    at_low = t == 0
    at_high = t == n_rad - 1
    shifted = jnp.where(spot_b % 2 == 0, spot_b, lax.rem(spot_b + LANES - 2, LANES))
    ghosted = jnp.where(shifted % 2 == 0, at_low.astype(jnp.int32), at_high.astype(jnp.int32))
    turn_at = (lane_b == shifted) & (ghosted == 1)
    angle = jnp.sum(
        jnp.where(turn_at, jnp.broadcast_to(column(pturn[...]), (border, LANES)), 0.0),
        axis=0, keepdims=True,
    )
    angle = jnp.broadcast_to(angle, (LEVELS, LANES))
    cosine, sine = jnp.cos(angle), jnp.sin(angle)

    radius = r_inner + (sub8.astype(jnp.float32) + 0.5) * ((1.0 - r_inner) / LEVELS)
    theta = math.pi / 4 + ((lane8 + t * LANES).astype(jnp.float32) + 0.5) * (
        math.pi / 2 / (LANES * n_rad)
    )
    inv_radius = 1.0 / radius
    inv_both = inv_radius / jnp.sin(theta)
    half_t = 0.5 * inv_radius
    mix_t = 0.1 * inv_radius * inv_radius
    half_p = 0.5 * inv_both
    mix_p = 0.1 * inv_both * inv_both
    centre = -2.0 * (0.1 + mix_t + mix_p)
    for i, value in enumerate((half_t, mix_t, half_p, mix_p, centre)):
        geo[i] = value

    pl.semaphore_wait(
        barrier,
        sources + n_rad - 1 + jnp.where(a > 0, 1, 0) + jnp.where(a < n_ang - 1, 1, 0),
    )

    for copy in fetches:
        copy.wait()
    loads = []
    for step in range(1, n_rad):
        to = lax.rem(t + step, n_rad)
        lanes = pl.ds(pl.multiple_of(to * LANES, LANES), LANES)
        for i, (src, dst) in enumerate((
            (first.at[0, :, lanes], land.at[0, own_rows, :]),
            (first.at[pl.ds(1, 3), :, lanes], land.at[pl.ds(1, 3), own_rows, :]),
            (first.at[pl.ds(4, 3), :, lanes], land.at[pl.ds(4, 3), own_rows, :]),
        )):
            loads.append(pltpu.make_async_remote_copy(
                src_ref=src, dst_ref=dst,
                send_sem=load_send.at[i, step], recv_sem=load_recv.at[i, step],
                device_id=at(mine, a, to), device_id_type=pl.DeviceIdType.MESH,
            ))
    for copy in loads:
        copy.start()

    def meta_copy(to):
        return pltpu.make_async_remote_copy(
            src_ref=meta_out, dst_ref=meta_in.at[a],
            send_sem=meta_send, recv_sem=meta_recv,
            device_id=at(other, to, t), device_id_type=pl.DeviceIdType.MESH,
        )

    def send_meta(to, carry):
        meta_copy(to).start()
        return carry

    lax.fori_loop(0, n_ang, send_meta, 0)
    pltpu.make_async_copy(meta_in, meta_in, meta_recv).wait()

    sub_l = lax.broadcasted_iota(jnp.int32, (LANES, LANES), 0)
    sub_c = lax.broadcasted_iota(jnp.int32, (cells, LANES), 0)

    def prepare(g, carry):
        table = jnp.sum(meta_in[pl.ds(g * per_tile, per_tile)], axis=0)
        device = table[0:1].astype(jnp.int32)
        at_phi = table[1:2].astype(jnp.int32)
        at_theta = table[2:3].astype(jnp.int32) - t * LANES
        hit = jnp.broadcast_to(device == a, (cells, LANES))
        near = hit & (sub_c == at_phi)
        far = hit & (sub_c == at_phi + 1)
        zero = jnp.zeros((cells, LANES), jnp.float32)
        w = [jnp.broadcast_to(table[3 + i:4 + i], (cells, LANES)) for i in range(4)]
        coef[g, 0] = jnp.where(near, w[0], jnp.where(far, w[2], zero))
        coef[g, 1] = jnp.where(near, w[1], jnp.where(far, w[3], zero))
        first = jnp.where(sub_l == at_theta, 1.0, 0.0).astype(jnp.bfloat16)
        second = jnp.where(sub_l == at_theta + 1, 1.0, 0.0).astype(jnp.bfloat16)
        for part in range(2):
            picker[g, pl.ds(part * LANES, LANES), pl.ds(0, LANES)] = first
            picker[g, pl.ds(part * LANES, LANES), pl.ds(LANES, LANES)] = second
        return carry

    if tiles == 1:
        prepare(0, 0)
    else:
        lax.fori_loop(0, tiles, prepare, 0)

    for copy in own:
        copy.wait()
    for copy in loads:
        copy.wait_recv()

    block_of = lane8 // border
    pair8 = lane8 // 2
    even = lane8 % 2 == 0
    first_lane = lane8 == 0
    last_lane = lane8 == LANES - 1
    first_level = sub8 == 0
    last_level = sub8 == LEVELS - 1

    def pack(k, f, value, packs):
        spot = border * (f % per_tile) + 2 * k + 1
        hit = pair8 == border // 2 * (f % per_tile) + k
        packs[f // per_tile] = jnp.where(
            hit, pltpu.roll(value, lax.rem(spot, LANES), 1), packs[f // per_tile]
        )

    def phi_copies(s):
        down = pltpu.make_async_remote_copy(
            src_ref=state.at[s, 0], dst_ref=phi_in.at[s, 1],
            send_sem=phi_send.at[s, 0], recv_sem=phi_recv.at[s, 1],
            device_id=at(mine, a, t) | {"ang": jnp.maximum(a - 1, 0)},
            device_id_type=pl.DeviceIdType.MESH,
        )
        up = pltpu.make_async_remote_copy(
            src_ref=state.at[s, cells - 1], dst_ref=phi_in.at[s, 0],
            send_sem=phi_send.at[s, 1], recv_sem=phi_recv.at[s, 0],
            device_id=at(mine, a, t) | {"ang": jnp.minimum(a + 1, n_ang - 1)},
            device_id_type=pl.DeviceIdType.MESH,
        )
        return down, up

    def theta_copies(s):
        down = pltpu.make_async_remote_copy(
            src_ref=theta_out.at[s], dst_ref=theta_in.at[s, 1],
            send_sem=theta_send.at[s, 0], recv_sem=theta_recv.at[s, 1],
            device_id=at(mine, a, jnp.maximum(t - 1, 0)),
            device_id_type=pl.DeviceIdType.MESH,
        )
        up = pltpu.make_async_remote_copy(
            src_ref=theta_out.at[s], dst_ref=theta_in.at[s, 0],
            send_sem=theta_send.at[s, 1], recv_sem=theta_recv.at[s, 0],
            device_id=at(mine, a, jnp.minimum(t + 1, n_rad - 1)),
            device_id_type=pl.DeviceIdType.MESH,
        )
        return down, up

    def over_copy(s, q):
        return pltpu.make_async_remote_copy(
            src_ref=over_out.at[s, q // 2], dst_ref=over_in.at[s, a * n_rad + t],
            send_sem=over_send.at[s], recv_sem=over_recv.at[s],
            device_id=at(other, q // 2, lax.rem(q, 2) * (n_rad - 1)),
            device_id_type=pl.DeviceIdType.MESH,
        )

    def send_all(s):
        theta_down, theta_up = theta_copies(s)
        phi_down, phi_up = phi_copies(s)
        for can, copy in (
            (t > 0, theta_down), (t < n_rad - 1, theta_up),
            (a > 0, phi_down), (a < n_ang - 1, phi_up),
        ):
            pl.when(can)(copy.start)

        def overset(g, carry):
            value = state[s].reshape(cells * FIELDS * LEVELS, LANES)
            head = value.astype(jnp.bfloat16)
            rest = (value - head.astype(jnp.float32)).astype(jnp.bfloat16)
            got = jnp.dot(
                jnp.concatenate([head, rest], axis=1), picker[g],
                preferred_element_type=jnp.float32,
            )
            ghosts = [None] * FIELDS
            for k in range(cells):
                near = jnp.broadcast_to(coef[g, 0, k:k + 1, :], (LEVELS, LANES))
                far = jnp.broadcast_to(coef[g, 1, k:k + 1, :], (LEVELS, LANES))
                for f in range(FIELDS):
                    at_row = (k * FIELDS + f) * LEVELS
                    piece = got[at_row:at_row + LEVELS]
                    term = piece[:, :LANES] * near + piece[:, LANES:] * far
                    ghosts[f] = term if k == 0 else ghosts[f] + term
            turned = [
                pltpu.roll(ghosts[f], border * (f % per_tile), 1) if f % per_tile else ghosts[f]
                for f in range(FIELDS)
            ]
            for j in range(per_tile):
                for half in range(2):
                    members = range(half * per_tile, min(FIELDS, (half + 1) * per_tile))
                    message = turned[members[0]]
                    for f in members:
                        message = jnp.where(
                            block_of == (f + j) % per_tile, turned[f], message
                        )
                    if j:
                        message = pltpu.roll(message, LANES - j * border, 1)
                    over_out[s, g * per_tile + j, half] = message
            for j in range(2 * per_tile):
                over_copy(s, g * 2 * per_tile + j).start()
            return carry

        if tiles == 1:
            overset(0, 0)
        else:
            lax.fori_loop(0, tiles, overset, 0)

    def inner(s):
        half_t, mix_t, half_p, mix_p, centre = [geo[i] for i in range(5)]

        def row(k, carry):
            u = [state[s, k, f] for f in range(FIELDS)]
            speed, pressure = point_values(u)
            stress, twist = {}, {}
            low_r, high_r = low_high(u, flux_of(u, speed, pressure, 0, stress, twist), 0.5, 0.1)
            low_t, high_t = low_high(u, flux_of(u, speed, pressure, 1, stress, twist), half_t, mix_t)
            low_p, high_p = low_high(u, flux_of(u, speed, pressure, 2, stress, twist), half_p, mix_p)
            for f in range(FIELDS):
                below = pltpu.roll(low_r[f], 1, 0)
                above = pltpu.roll(high_r[f], LEVELS - 1, 0)
                below = jnp.where(first_level, wall[f] * high_r[f], below)
                above = jnp.where(last_level, wall[f] * low_r[f], above)
                left = jnp.where(first_lane, 0.0, pltpu.roll(low_t[f], 1, 1))
                right = jnp.where(last_lane, 0.0, pltpu.roll(high_t[f], LANES - 1, 1))
                value = (below + above) + (left + right)
                if mixing[f] != 0.0:
                    value = value + centre * u[f]
                slope[k, f] = value
                x_low[k + 1, f] = low_p[f]
                x_high[k + 1, f] = high_p[f]
            return carry

        lax.fori_loop(0, cells, row, 0, unroll=4)

    def halos(s):
        half_t, mix_t, half_p, mix_p, centre = [geo[i] for i in range(5)]
        phi_down, phi_up = phi_copies(s)
        theta_down, theta_up = theta_copies(s)

        def beside(side):
            u = [phi_in[s, side, f] for f in range(FIELDS)]
            speed, pressure = point_values(u)
            low, high = low_high(u, flux_of(u, speed, pressure, 2, {}, {}), half_p, mix_p)
            for f in range(FIELDS):
                if side == 0:
                    x_low[0, f] = low[f]
                else:
                    x_high[cells + 1, f] = high[f]

        @pl.when(a > 0)
        def _():
            phi_up.wait_recv()
            beside(0)

        @pl.when(a == 0)
        def _():
            for f in range(FIELDS):
                x_low[0, f] = wall[f] * x_high[1, f]

        @pl.when(a < n_ang - 1)
        def _():
            phi_down.wait_recv()
            beside(1)

        @pl.when(a == n_ang - 1)
        def _():
            for f in range(FIELDS):
                x_high[cells + 1, f] = wall[f] * x_low[cells, f]

        @pl.when(t > 0)
        def _():
            theta_up.wait_recv()

        @pl.when(t < n_rad - 1)
        def _():
            theta_down.wait_recv()

        @pl.when(at_low | at_high)
        def _():
            pltpu.make_async_copy(over_in.at[s], over_in.at[s], over_recv.at[s]).wait()
            ghost = jnp.sum(over_in[s], axis=0)
            @pl.when(at_low)
            def _():
                theta_in[s, 0] = ghost

            @pl.when(at_high)
            def _():
                theta_in[s, 1] = ghost

        both = [
            jnp.where(even, theta_in[s, 0, h], pltpu.roll(theta_in[s, 1, h], LANES - 2, 1))
            for h in range(2)
        ]
        u = []
        for f in range(FIELDS):
            away = border * (f % per_tile)
            value = both[f // per_tile]
            u.append(pltpu.roll(value, LANES - away, 1) if away else value)
        for f in (2, 5):
            u[f], u[f + 1] = cosine * u[f] + sine * u[f + 1], cosine * u[f + 1] - sine * u[f]
        speed, pressure = point_values(u)
        signed = jnp.where(even, half_t, -half_t)
        edge, _ = low_high(u, flux_of(u, speed, pressure, 1, {}, {}), signed, mix_t)
        return edge

    def tend(k, f, edge):
        ends = pltpu.roll(edge[f], lax.rem(LANES - 2 * k, LANES), 1)
        ends = jnp.where(outer_lanes, ends, 0.0)
        return (slope[k, f] + ends) + (x_low[k, f] + x_high[k + 2, f])

    zero8 = jnp.zeros((LEVELS, LANES), jnp.float32)
    outer_lanes = first_lane | last_lane

    def enter(k, packs):
        packs = list(packs)
        for f in range(FIELDS):
            value = land[f, pl.ds(k, LEVELS, stride=cells), :]
            state[0, k, f] = value
            total[k, f] = value
            pack(k, f, value, packs)
        return tuple(packs)

    def keep(s, packs):
        for half in range(2):
            theta_out[s, half] = packs[half]

    keep(0, lax.fori_loop(0, cells, enter, (zero8, zero8), unroll=4))

    def stage(s, carry):
        send_all(s)
        inner(s)
        edge = halos(s)
        step_on = jnp.where(s < 2, ahead[0], ahead[2])
        weight = jnp.where((s == 0) | (s == 3), share[0], share[1])

        def advance(k, packs):
            packs = list(packs)
            for f in range(FIELDS):
                now = tend(k, f, edge)
                value = state[0, k, f] + step_on * now
                state[s + 1, k, f] = value
                pack(k, f, value, packs)
                total[k, f] = total[k, f] + weight * now
            return tuple(packs)

        keep(s + 1, lax.fori_loop(0, cells, advance, (zero8, zero8), unroll=4))
        return carry

    lax.fori_loop(0, 4, stage, 0)

    def leave(k, carry):
        for f in range(FIELDS):
            staged[f, pl.ds(k, LEVELS, stride=cells), :] = total[k, f]
        return carry

    lax.fori_loop(0, cells, leave, 0, unroll=4)

    gives = []
    for step in range(1, n_rad):
        to = lax.rem(t + step, n_rad)
        there = pl.ds(pl.multiple_of(to * rows, rows), rows)
        for i, (src, dst) in enumerate((
            (staged.at[0, there, :], oden.at[:, own_lanes]),
            (staged.at[pl.ds(1, 3), there, :], omom.at[:, :, own_lanes]),
            (staged.at[pl.ds(4, 3), there, :], omag.at[:, :, own_lanes]),
        )):
            gives.append(pltpu.make_async_remote_copy(
                src_ref=src, dst_ref=dst,
                send_sem=give_send.at[i, step], recv_sem=give_recv.at[i, step],
                device_id=at(mine, a, to), device_id_type=pl.DeviceIdType.MESH,
            ))
    for copy in gives:
        copy.start()
    keeps = [
        pltpu.make_async_copy(staged.at[0, own_rows, :], oden.at[:, own_lanes], own_sem.at[0]),
        pltpu.make_async_copy(staged.at[pl.ds(1, 3), own_rows, :], omom.at[:, :, own_lanes], own_sem.at[1]),
        pltpu.make_async_copy(staged.at[pl.ds(4, 3), own_rows, :], omag.at[:, :, own_lanes], own_sem.at[2]),
    ]
    for copy in keeps:
        copy.start()

    for copy in loads:
        copy.wait_send()
    pltpu.make_async_copy(meta_in, meta_in, meta_send).wait()
    for s in range(4):
        phi_down, phi_up = phi_copies(s)
        theta_down, theta_up = theta_copies(s)
        for can, copy in (
            (t > 0, theta_down), (t < n_rad - 1, theta_up),
            (a > 0, phi_down), (a < n_ang - 1, phi_up),
        ):
            pl.when(can)(copy.wait_send)
        for _ in range(2):
            pltpu.make_async_copy(over_out.at[s], over_out.at[s], over_send.at[s]).wait()
    for copy in keeps:
        copy.wait()
    for copy in gives:
        copy.wait()


def hand_over(one, two, three, out_one, out_two, out_three, sems):
    copies = [
        pltpu.make_async_copy(src, dst, sems.at[i])
        for i, (src, dst) in enumerate(
            [(one, out_one)]
            + [(two.at[c], out_two.at[c]) for c in range(3)]
            + [(three.at[c], out_three.at[c]) for c in range(3)]
        )
    ]
    for copy in copies:
        copy.start()
    for copy in copies:
        copy.wait()


def body(density, momentum, magnetic, partner_device, partner_phi, partner_theta, partner_weight,
         border_turn):
    _, rows_r, cells, n_theta = density.shape
    border = partner_phi.shape[1]
    n_ang, n_rad = lax.axis_size("ang"), lax.axis_size("rad")
    rows = rows_r * cells
    assert rows_r * n_rad == LEVELS and n_theta == LANES * n_rad and n_rad > 1
    assert border * 4 == LANES and n_ang % (LANES // border) == 0 and border == 2 * cells
    f32 = jnp.float32
    tiles = n_ang * border // LANES
    sources = n_ang * n_rad
    vmem = pltpu.VMEM
    dma = pltpu.SemaphoreType.DMA
    spaces = [pl.BlockSpec(memory_space=pltpu.HBM)] * 8
    outs = pl.pallas_call(
        functools.partial(kernel, (n_ang, n_rad, rows, cells, border)),
        out_shape=(
            jax.ShapeDtypeStruct((rows, n_theta), f32),
            jax.ShapeDtypeStruct((3, rows, n_theta), f32),
            jax.ShapeDtypeStruct((3, rows, n_theta), f32),
        ),
        in_specs=spaces,
        out_specs=[pl.BlockSpec(memory_space=pl.ANY)] * 3,
        scratch_shapes=[
            vmem((1, border), jnp.int32), vmem((1, border), jnp.int32),
            vmem((1, border), jnp.int32), vmem((4, border), f32), vmem((1, border), f32),
            vmem((FIELDS, rows, n_theta), f32), dma((3,)),
            vmem((FIELDS, LEVELS * cells, LANES), f32),
            vmem((FIELDS, LEVELS * cells, LANES), f32),
            vmem((5, cells, FIELDS, LEVELS, LANES), f32),
            vmem((cells, FIELDS, LEVELS, LANES), f32),
            vmem((cells, FIELDS, LEVELS, LANES), f32),
            vmem((cells + 2, FIELDS, LEVELS, LANES), f32),
            vmem((cells + 2, FIELDS, LEVELS, LANES), f32),
            vmem((5, LEVELS, LANES), f32),
            vmem((4, 2, FIELDS, LEVELS, LANES), f32),
            vmem((5, 2, LEVELS, LANES), f32),
            vmem((4, 2, 2, LEVELS, LANES), f32),
            vmem((4, n_ang, 2, LEVELS, LANES), f32),
            vmem((4, sources, 2, LEVELS, LANES), f32),
            vmem((LEVELS, LANES), f32),
            vmem((n_ang, LEVELS, LANES), f32),
            vmem((tiles, 2, cells, LANES), f32),
            vmem((tiles, 2 * LANES, 2 * LANES), jnp.bfloat16),
            dma((5,)), dma((3,)), dma((3, n_rad)), dma((3, n_rad)), dma((3, n_rad)), dma((3, n_rad)),
            dma, dma, dma((4, 2)), dma((4, 2)), dma((4, 2)), dma((4, 2)), dma((4,)), dma((4,)),
        ],
        compiler_params=pltpu.CompilerParams(
            collective_id=0, has_side_effects=True, vmem_limit_bytes=vmem_bytes
        ),
    )(
        *[pltpu.with_memory_space_constraint(x, pltpu.HBM) for x in (
        density.reshape(rows, n_theta),
        momentum.reshape(3, rows, n_theta),
        magnetic.reshape(3, rows, n_theta),
        partner_device.reshape(1, border),
        partner_phi, partner_theta,
        partner_weight.reshape(border, 4).T,
        border_turn,
        )]
    )
    outs = pl.pallas_call(
        hand_over,
        out_shape=tuple(jax.ShapeDtypeStruct(o.shape, f32) for o in outs),
        in_specs=[pl.BlockSpec(memory_space=pl.ANY)] * 3,
        out_specs=[pl.BlockSpec(memory_space=pltpu.HBM)] * 3,
        scratch_shapes=[dma((FIELDS,))],
        compiler_params=pltpu.CompilerParams(vmem_limit_bytes=vmem_bytes),
    )(*outs)
    return (
        outs[0].reshape(density.shape),
        outs[1].reshape(momentum.shape),
        outs[2].reshape(magnetic.shape),
    )


def solution(mesh):
    in_specs = (
        P("panel", "rad", "ang", None),
        P("panel", None, "rad", "ang", None),
        P("panel", None, "rad", "ang", None),
        P("panel", "ang", None),
        P("panel", "ang"),
        P("panel", "ang"),
        P("panel", "ang", None),
        P("panel", "ang"),
    )
    out_specs = (
        P("panel", "rad", "ang", None),
        P("panel", None, "rad", "ang", None),
        P("panel", None, "rad", "ang", None),
    )
    return jax.shard_map(body, mesh=mesh, in_specs=in_specs, out_specs=out_specs, check_vma=False)
```

```python
import functools
import math

import jax
import jax.numpy as jnp
from jax import lax
from jax.experimental import pallas as pl
from jax.experimental.pallas import tpu as pltpu
from jax.sharding import PartitionSpec as P

time_step = 0.15
mixing = (0.0, 0.1, 0.1, 0.1, 0.1, 0.1, 0.1)
wall = (1.0, -1.0, -1.0, -1.0, 1.0, 1.0, 1.0)
r_inner = 0.35
FIELDS = 7
LANES = 128
LEVELS = 8
vmem_bytes = 32 * 1024 * 1024
ahead = (0.5 * time_step, 0.5 * time_step, time_step)
share = (time_step / 6.0, time_step / 3.0, time_step / 3.0, time_step / 6.0)


def point_values(u):
    rate = 1.0 / u[0]
    speed = [u[1 + c] * rate for c in range(3)]
    pressure = u[0] + 0.5 * (u[4] * u[4] + u[5] * u[5] + u[6] * u[6])
    return speed, pressure


def flux_of(u, speed, pressure, d, stress, twist):
    out = [u[1 + d]]
    for c in range(3):
        key = (min(c, d), max(c, d))
        if key not in stress:
            term = u[1 + c] * speed[d] - u[4 + c] * u[4 + d]
            stress[key] = term + pressure if c == d else term
        out.append(stress[key])
    for c in range(3):
        if c == d:
            out.append(None)
            continue
        key = (min(c, d), max(c, d))
        if key not in twist:
            low, high = key
            twist[key] = speed[high] * u[4 + low] - u[4 + high] * speed[low]
        out.append(twist[key] if c == key[0] else -twist[key])
    return out


def low_high(u, flux, half, mix):
    low, high = [], []
    for f in range(FIELDS):
        carried = None if flux[f] is None else half * flux[f]
        spread = None if mixing[f] == 0.0 else mix * u[f]
        if carried is None:
            low.append(spread)
            high.append(spread)
        elif spread is None:
            low.append(carried)
            high.append(-carried)
        else:
            low.append(spread + carried)
            high.append(spread - carried)
    return low, high


def kernel(
    sizes,
    den, mom, mag, pdev_hbm, pphi_hbm, ptheta_hbm, pweight_hbm, pturn_hbm,
    oden, omom, omag,
    pdev, pphi, ptheta, pweight, pturn, first, fetch_sem,
    land, staged, state, total, slope, x_low, x_high, geo,
    phi_in, theta_out, theta_in, over_out, over_in,
    meta_out, meta_in, coef, picker,
    small_sem, own_sem, load_send, load_recv, give_send, give_recv,
    meta_send, meta_recv, phi_send, phi_recv, theta_send, theta_recv,
    over_send, over_recv,
):
    n_ang, n_rad, rows, cells, border = sizes
    side_rows = border // 2
    per_tile = LANES // border
    tiles = n_ang // per_tile
    sources = n_ang * n_rad
    mine = lax.axis_index("panel")
    a = lax.axis_index("ang")
    t = lax.axis_index("rad")
    other = 1 - mine

    def at(panel, ang, rad):
        return {"panel": panel, "ang": ang, "rad": rad}

    small = [
        pltpu.make_async_copy(src, dst, small_sem.at[i])
        for i, (src, dst) in enumerate((
            (pdev_hbm, pdev), (pphi_hbm, pphi), (ptheta_hbm, ptheta),
            (pweight_hbm, pweight), (pturn_hbm, pturn),
        ))
    ]
    for copy in small:
        copy.start()
    fetches = [
        pltpu.make_async_copy(den, first.at[0], fetch_sem.at[0]),
        pltpu.make_async_copy(mom, first.at[pl.ds(1, 3)], fetch_sem.at[1]),
        pltpu.make_async_copy(mag, first.at[pl.ds(4, 3)], fetch_sem.at[2]),
    ]
    for copy in fetches:
        copy.start()

    barrier = pltpu.get_barrier_semaphore()

    def greet(i, carry):
        pl.semaphore_signal(
            barrier, inc=1,
            device_id=at(other, i // n_rad, lax.rem(i, n_rad)),
            device_id_type=pl.DeviceIdType.MESH,
        )
        return carry

    lax.fori_loop(0, sources, greet, 0)
    for step in range(1, n_rad):
        pl.semaphore_signal(
            barrier, inc=1, device_id=at(mine, a, lax.rem(t + step, n_rad)),
            device_id_type=pl.DeviceIdType.MESH,
        )

    @pl.when(a > 0)
    def _():
        pl.semaphore_signal(
            barrier, inc=1, device_id=at(mine, a - 1, t), device_id_type=pl.DeviceIdType.MESH
        )

    @pl.when(a < n_ang - 1)
    def _():
        pl.semaphore_signal(
            barrier, inc=1, device_id=at(mine, a + 1, t), device_id_type=pl.DeviceIdType.MESH
        )

    own_rows = pl.ds(pl.multiple_of(t * rows, rows), rows)
    own_lanes = pl.ds(pl.multiple_of(t * LANES, LANES), LANES)
    own = [
        pltpu.make_async_copy(den.at[:, own_lanes], land.at[0, own_rows, :], own_sem.at[0]),
        pltpu.make_async_copy(mom.at[:, :, own_lanes], land.at[pl.ds(1, 3), own_rows, :], own_sem.at[1]),
        pltpu.make_async_copy(mag.at[:, :, own_lanes], land.at[pl.ds(4, 3), own_rows, :], own_sem.at[2]),
    ]
    for copy in own:
        copy.start()

    sub8 = lax.broadcasted_iota(jnp.int32, (LEVELS, LANES), 0)
    lane8 = lax.broadcasted_iota(jnp.int32, (LEVELS, LANES), 1)
    sub_b = lax.broadcasted_iota(jnp.int32, (border, LANES), 0)
    lane_b = lax.broadcasted_iota(jnp.int32, (border, LANES), 1)
    square = (
        lax.broadcasted_iota(jnp.int32, (border, border), 0)
        == lax.broadcasted_iota(jnp.int32, (border, border), 1)
    )

    def column(row):
        wide = jnp.broadcast_to(row, (border, border))
        return jnp.sum(jnp.where(square, wide, 0.0), axis=1, keepdims=True)

    spot_b = jnp.where(sub_b < side_rows, 2 * sub_b, 2 * sub_b - (border - 1))
    place = lane_b == spot_b + border * lax.rem(a, per_tile)
    for copy in small:
        copy.wait()
    columns = [
        column(pdev[...].astype(jnp.float32)),
        column(pphi[...].astype(jnp.float32)),
        column(ptheta[...].astype(jnp.float32)),
    ] + [column(pweight[i:i + 1, :]) for i in range(4)]
    meta_out[...] = jnp.zeros_like(meta_out)
    for i, col in enumerate(columns):
        meta_out[i:i + 1, :] = jnp.sum(
            jnp.where(place, jnp.broadcast_to(col, (border, LANES)), 0.0), axis=0, keepdims=True
        )

    at_low = t == 0
    at_high = t == n_rad - 1
    shifted = jnp.where(spot_b % 2 == 0, spot_b, lax.rem(spot_b + LANES - 2, LANES))
    ghosted = jnp.where(shifted % 2 == 0, at_low.astype(jnp.int32), at_high.astype(jnp.int32))
    turn_at = (lane_b == shifted) & (ghosted == 1)
    angle = jnp.sum(
        jnp.where(turn_at, jnp.broadcast_to(column(pturn[...]), (border, LANES)), 0.0),
        axis=0, keepdims=True,
    )
    angle = jnp.broadcast_to(angle, (LEVELS, LANES))
    cosine, sine = jnp.cos(angle), jnp.sin(angle)

    radius = r_inner + (sub8.astype(jnp.float32) + 0.5) * ((1.0 - r_inner) / LEVELS)
    theta = math.pi / 4 + ((lane8 + t * LANES).astype(jnp.float32) + 0.5) * (
        math.pi / 2 / (LANES * n_rad)
    )
    inv_radius = 1.0 / radius
    inv_both = inv_radius / jnp.sin(theta)
    half_t = 0.5 * inv_radius
    mix_t = 0.1 * inv_radius * inv_radius
    half_p = 0.5 * inv_both
    mix_p = 0.1 * inv_both * inv_both
    centre = -2.0 * (0.1 + mix_t + mix_p)
    for i, value in enumerate((half_t, mix_t, half_p, mix_p, centre)):
        geo[i] = value

    pl.semaphore_wait(
        barrier,
        sources + n_rad - 1 + jnp.where(a > 0, 1, 0) + jnp.where(a < n_ang - 1, 1, 0),
    )

    for copy in fetches:
        copy.wait()
    loads = []
    for step in range(1, n_rad):
        to = lax.rem(t + step, n_rad)
        lanes = pl.ds(pl.multiple_of(to * LANES, LANES), LANES)
        for i, (src, dst) in enumerate((
            (first.at[0, :, lanes], land.at[0, own_rows, :]),
            (first.at[pl.ds(1, 3), :, lanes], land.at[pl.ds(1, 3), own_rows, :]),
            (first.at[pl.ds(4, 3), :, lanes], land.at[pl.ds(4, 3), own_rows, :]),
        )):
            loads.append(pltpu.make_async_remote_copy(
                src_ref=src, dst_ref=dst,
                send_sem=load_send.at[i, step], recv_sem=load_recv.at[i, step],
                device_id=at(mine, a, to), device_id_type=pl.DeviceIdType.MESH,
            ))
    for copy in loads:
        copy.start()

    def meta_copy(to):
        return pltpu.make_async_remote_copy(
            src_ref=meta_out, dst_ref=meta_in.at[a],
            send_sem=meta_send, recv_sem=meta_recv,
            device_id=at(other, to, t), device_id_type=pl.DeviceIdType.MESH,
        )

    def send_meta(to, carry):
        meta_copy(to).start()
        return carry

    lax.fori_loop(0, n_ang, send_meta, 0)
    pltpu.make_async_copy(meta_in, meta_in, meta_recv).wait()

    sub_l = lax.broadcasted_iota(jnp.int32, (LANES, LANES), 0)
    sub_c = lax.broadcasted_iota(jnp.int32, (cells, LANES), 0)

    def prepare(g, carry):
        table = jnp.sum(meta_in[pl.ds(g * per_tile, per_tile)], axis=0)
        device = table[0:1].astype(jnp.int32)
        at_phi = table[1:2].astype(jnp.int32)
        at_theta = table[2:3].astype(jnp.int32) - t * LANES
        hit = jnp.broadcast_to(device == a, (cells, LANES))
        near = hit & (sub_c == at_phi)
        far = hit & (sub_c == at_phi + 1)
        zero = jnp.zeros((cells, LANES), jnp.float32)
        w = [jnp.broadcast_to(table[3 + i:4 + i], (cells, LANES)) for i in range(4)]
        coef[g, 0] = jnp.where(near, w[0], jnp.where(far, w[2], zero))
        coef[g, 1] = jnp.where(near, w[1], jnp.where(far, w[3], zero))
        first = jnp.where(sub_l == at_theta, 1.0, 0.0).astype(jnp.bfloat16)
        second = jnp.where(sub_l == at_theta + 1, 1.0, 0.0).astype(jnp.bfloat16)
        for part in range(2):
            picker[g, pl.ds(part * LANES, LANES), pl.ds(0, LANES)] = first
            picker[g, pl.ds(part * LANES, LANES), pl.ds(LANES, LANES)] = second
        return carry

    if tiles == 1:
        prepare(0, 0)
    else:
        lax.fori_loop(0, tiles, prepare, 0)

    for copy in own:
        copy.wait()
    for copy in loads:
        copy.wait_recv()

    block_of = lane8 // border
    pair8 = lane8 // 2
    even = lane8 % 2 == 0
    first_lane = lane8 == 0
    last_lane = lane8 == LANES - 1
    first_level = sub8 == 0
    last_level = sub8 == LEVELS - 1

    def pack(k, f, value, packs):
        spot = border * (f % per_tile) + 2 * k + 1
        hit = pair8 == border // 2 * (f % per_tile) + k
        packs[f // per_tile] = jnp.where(
            hit, pltpu.roll(value, lax.rem(spot, LANES), 1), packs[f // per_tile]
        )

    def phi_copies(s):
        down = pltpu.make_async_remote_copy(
            src_ref=state.at[s, 0], dst_ref=phi_in.at[s, 1],
            send_sem=phi_send.at[s, 0], recv_sem=phi_recv.at[s, 1],
            device_id=at(mine, a, t) | {"ang": jnp.maximum(a - 1, 0)},
            device_id_type=pl.DeviceIdType.MESH,
        )
        up = pltpu.make_async_remote_copy(
            src_ref=state.at[s, cells - 1], dst_ref=phi_in.at[s, 0],
            send_sem=phi_send.at[s, 1], recv_sem=phi_recv.at[s, 0],
            device_id=at(mine, a, t) | {"ang": jnp.minimum(a + 1, n_ang - 1)},
            device_id_type=pl.DeviceIdType.MESH,
        )
        return down, up

    def theta_copies(s):
        down = pltpu.make_async_remote_copy(
            src_ref=theta_out.at[s], dst_ref=theta_in.at[s, 1],
            send_sem=theta_send.at[s, 0], recv_sem=theta_recv.at[s, 1],
            device_id=at(mine, a, jnp.maximum(t - 1, 0)),
            device_id_type=pl.DeviceIdType.MESH,
        )
        up = pltpu.make_async_remote_copy(
            src_ref=theta_out.at[s], dst_ref=theta_in.at[s, 0],
            send_sem=theta_send.at[s, 1], recv_sem=theta_recv.at[s, 0],
            device_id=at(mine, a, jnp.minimum(t + 1, n_rad - 1)),
            device_id_type=pl.DeviceIdType.MESH,
        )
        return down, up

    def over_copy(s, q):
        return pltpu.make_async_remote_copy(
            src_ref=over_out.at[s, q], dst_ref=over_in.at[s, a * n_rad + t],
            send_sem=over_send.at[s], recv_sem=over_recv.at[s],
            device_id=at(other, q // 2, lax.rem(q, 2) * (n_rad - 1)),
            device_id_type=pl.DeviceIdType.MESH,
        )

    def send_all(s):
        theta_down, theta_up = theta_copies(s)
        phi_down, phi_up = phi_copies(s)
        for can, copy in (
            (t > 0, theta_down), (t < n_rad - 1, theta_up),
            (a > 0, phi_down), (a < n_ang - 1, phi_up),
        ):
            pl.when(can)(copy.start)

        def overset(g, carry):
            value = state[s].reshape(cells * FIELDS * LEVELS, LANES)
            head = value.astype(jnp.bfloat16)
            rest = (value - head.astype(jnp.float32)).astype(jnp.bfloat16)
            got = jnp.dot(
                jnp.concatenate([head, rest], axis=1), picker[g],
                preferred_element_type=jnp.float32,
            )
            ghosts = [None] * FIELDS
            for k in range(cells):
                near = jnp.broadcast_to(coef[g, 0, k:k + 1, :], (LEVELS, LANES))
                far = jnp.broadcast_to(coef[g, 1, k:k + 1, :], (LEVELS, LANES))
                for f in range(FIELDS):
                    at_row = (k * FIELDS + f) * LEVELS
                    piece = got[at_row:at_row + LEVELS]
                    term = piece[:, :LANES] * near + piece[:, LANES:] * far
                    ghosts[f] = term if k == 0 else ghosts[f] + term
            turned = [
                pltpu.roll(ghosts[f], border * (f % per_tile), 1) if f % per_tile else ghosts[f]
                for f in range(FIELDS)
            ]
            for j in range(per_tile):
                pair = []
                for half in range(2):
                    members = range(half * per_tile, min(FIELDS, (half + 1) * per_tile))
                    message = turned[members[0]]
                    for f in members:
                        message = jnp.where(
                            block_of == (f + j) % per_tile, turned[f], message
                        )
                    if j:
                        message = pltpu.roll(message, LANES - j * border, 1)
                    pair.append(message)
                at_pair = 2 * (g * per_tile + j)
                over_out[s, at_pair] = jnp.where(even, pair[0], pltpu.roll(pair[1], 1, 1))
                over_out[s, at_pair + 1] = jnp.where(
                    even, pltpu.roll(pair[0], LANES - 1, 1), pair[1]
                )
            for j in range(2 * per_tile):
                over_copy(s, g * 2 * per_tile + j).start()
            return carry

        if tiles == 1:
            overset(0, 0)
        else:
            lax.fori_loop(0, tiles, overset, 0)

    def inner(s):
        half_t, mix_t, half_p, mix_p, centre = [geo[i] for i in range(5)]

        def row(k, carry):
            u = [state[s, k, f] for f in range(FIELDS)]
            speed, pressure = point_values(u)
            stress, twist = {}, {}
            low_r, high_r = low_high(u, flux_of(u, speed, pressure, 0, stress, twist), 0.5, 0.1)
            low_t, high_t = low_high(u, flux_of(u, speed, pressure, 1, stress, twist), half_t, mix_t)
            low_p, high_p = low_high(u, flux_of(u, speed, pressure, 2, stress, twist), half_p, mix_p)
            for f in range(FIELDS):
                below = pltpu.roll(low_r[f], 1, 0)
                above = pltpu.roll(high_r[f], LEVELS - 1, 0)
                below = jnp.where(first_level, wall[f] * high_r[f], below)
                above = jnp.where(last_level, wall[f] * low_r[f], above)
                left = jnp.where(first_lane, 0.0, pltpu.roll(low_t[f], 1, 1))
                right = jnp.where(last_lane, 0.0, pltpu.roll(high_t[f], LANES - 1, 1))
                value = (below + above) + (left + right)
                if mixing[f] != 0.0:
                    value = value + centre * u[f]
                slope[k, f] = value
                x_low[k + 1, f] = low_p[f]
                x_high[k + 1, f] = high_p[f]
            return carry

        lax.fori_loop(0, cells, row, 0, unroll=8)

    def halos(s):
        half_t, mix_t, half_p, mix_p, centre = [geo[i] for i in range(5)]
        phi_down, phi_up = phi_copies(s)
        theta_down, theta_up = theta_copies(s)

        def beside(side):
            u = [phi_in[s, side, f] for f in range(FIELDS)]
            speed, pressure = point_values(u)
            low, high = low_high(u, flux_of(u, speed, pressure, 2, {}, {}), half_p, mix_p)
            for f in range(FIELDS):
                if side == 0:
                    x_low[0, f] = low[f]
                else:
                    x_high[cells + 1, f] = high[f]

        @pl.when(a > 0)
        def _():
            phi_up.wait_recv()
            beside(0)

        @pl.when(a == 0)
        def _():
            for f in range(FIELDS):
                x_low[0, f] = wall[f] * x_high[1, f]

        @pl.when(a < n_ang - 1)
        def _():
            phi_down.wait_recv()
            beside(1)

        @pl.when(a == n_ang - 1)
        def _():
            for f in range(FIELDS):
                x_high[cells + 1, f] = wall[f] * x_low[cells, f]

        @pl.when(t > 0)
        def _():
            theta_up.wait_recv()

        @pl.when(t < n_rad - 1)
        def _():
            theta_down.wait_recv()

        @pl.when(at_low | at_high)
        def _():
            pltpu.make_async_copy(over_in.at[s], over_in.at[s], over_recv.at[s]).wait()
            ghost = jnp.sum(over_in[s], axis=0)
            @pl.when(at_low)
            def _():
                theta_in[s, 0, 0] = ghost
                theta_in[s, 0, 1] = pltpu.roll(ghost, LANES - 1, 1)

            @pl.when(at_high)
            def _():
                theta_in[s, 1, 0] = pltpu.roll(ghost, 1, 1)
                theta_in[s, 1, 1] = ghost

        both = [
            jnp.where(even, theta_in[s, 0, h], pltpu.roll(theta_in[s, 1, h], LANES - 2, 1))
            for h in range(2)
        ]
        u = []
        for f in range(FIELDS):
            away = border * (f % per_tile)
            value = both[f // per_tile]
            u.append(pltpu.roll(value, LANES - away, 1) if away else value)
        for f in (2, 5):
            u[f], u[f + 1] = cosine * u[f] + sine * u[f + 1], cosine * u[f + 1] - sine * u[f]
        speed, pressure = point_values(u)
        signed = jnp.where(even, half_t, -half_t)
        edge, _ = low_high(u, flux_of(u, speed, pressure, 1, {}, {}), signed, mix_t)
        return edge

    def tend(k, f, edge):
        ends = pltpu.roll(edge[f], lax.rem(LANES - 2 * k, LANES), 1)
        ends = jnp.where(outer_lanes, ends, 0.0)
        return (slope[k, f] + ends) + (x_low[k, f] + x_high[k + 2, f])

    zero8 = jnp.zeros((LEVELS, LANES), jnp.float32)
    outer_lanes = first_lane | last_lane

    def enter(k, packs):
        packs = list(packs)
        for f in range(FIELDS):
            value = land[f, pl.ds(k, LEVELS, stride=cells), :]
            state[0, k, f] = value
            total[k, f] = value
            pack(k, f, value, packs)
        return tuple(packs)

    def keep(s, packs):
        for half in range(2):
            theta_out[s, half] = packs[half]

    keep(0, lax.fori_loop(0, cells, enter, (zero8, zero8), unroll=True))

    def stage(s, carry):
        send_all(s)
        inner(s)
        edge = halos(s)
        step_on = jnp.where(s < 2, ahead[0], ahead[2])
        weight = jnp.where((s == 0) | (s == 3), share[0], share[1])

        def advance(k, packs):
            packs = list(packs)
            for f in range(FIELDS):
                now = tend(k, f, edge)
                value = state[0, k, f] + step_on * now
                state[s + 1, k, f] = value
                pack(k, f, value, packs)
                total[k, f] = total[k, f] + weight * now
            return tuple(packs)

        keep(s + 1, lax.fori_loop(0, cells, advance, (zero8, zero8), unroll=True))
        return carry

    lax.fori_loop(0, 4, stage, 0)

    def leave(k, carry):
        for f in range(FIELDS):
            staged[f, pl.ds(k, LEVELS, stride=cells), :] = total[k, f]
        return carry

    lax.fori_loop(0, cells, leave, 0, unroll=4)

    gives = []
    for step in range(1, n_rad):
        to = lax.rem(t + step, n_rad)
        there = pl.ds(pl.multiple_of(to * rows, rows), rows)
        for i, (src, dst) in enumerate((
            (staged.at[0, there, :], oden.at[:, own_lanes]),
            (staged.at[pl.ds(1, 3), there, :], omom.at[:, :, own_lanes]),
            (staged.at[pl.ds(4, 3), there, :], omag.at[:, :, own_lanes]),
        )):
            gives.append(pltpu.make_async_remote_copy(
                src_ref=src, dst_ref=dst,
                send_sem=give_send.at[i, step], recv_sem=give_recv.at[i, step],
                device_id=at(mine, a, to), device_id_type=pl.DeviceIdType.MESH,
            ))
    for copy in gives:
        copy.start()
    keeps = [
        pltpu.make_async_copy(staged.at[0, own_rows, :], oden.at[:, own_lanes], own_sem.at[0]),
        pltpu.make_async_copy(staged.at[pl.ds(1, 3), own_rows, :], omom.at[:, :, own_lanes], own_sem.at[1]),
        pltpu.make_async_copy(staged.at[pl.ds(4, 3), own_rows, :], omag.at[:, :, own_lanes], own_sem.at[2]),
    ]
    for copy in keeps:
        copy.start()

    for copy in loads:
        copy.wait_send()
    pltpu.make_async_copy(meta_in, meta_in, meta_send).wait()
    for s in range(4):
        phi_down, phi_up = phi_copies(s)
        theta_down, theta_up = theta_copies(s)
        for can, copy in (
            (t > 0, theta_down), (t < n_rad - 1, theta_up),
            (a > 0, phi_down), (a < n_ang - 1, phi_up),
        ):
            pl.when(can)(copy.wait_send)
        pltpu.make_async_copy(over_out.at[s], over_out.at[s], over_send.at[s]).wait()
    for copy in keeps:
        copy.wait()
    for copy in gives:
        copy.wait()


def hand_over(one, two, three, out_one, out_two, out_three, sems):
    copies = [
        pltpu.make_async_copy(src, dst, sems.at[i])
        for i, (src, dst) in enumerate(
            [(one, out_one)]
            + [(two.at[c], out_two.at[c]) for c in range(3)]
            + [(three.at[c], out_three.at[c]) for c in range(3)]
        )
    ]
    for copy in copies:
        copy.start()
    for copy in copies:
        copy.wait()


def body(density, momentum, magnetic, partner_device, partner_phi, partner_theta, partner_weight,
         border_turn):
    _, rows_r, cells, n_theta = density.shape
    border = partner_phi.shape[1]
    n_ang, n_rad = lax.axis_size("ang"), lax.axis_size("rad")
    rows = rows_r * cells
    assert rows_r * n_rad == LEVELS and n_theta == LANES * n_rad and n_rad > 1
    assert border * 4 == LANES and n_ang % (LANES // border) == 0 and border == 2 * cells
    f32 = jnp.float32
    tiles = n_ang * border // LANES
    sources = n_ang * n_rad
    vmem = pltpu.VMEM
    dma = pltpu.SemaphoreType.DMA
    spaces = [pl.BlockSpec(memory_space=pltpu.HBM)] * 8
    outs = pl.pallas_call(
        functools.partial(kernel, (n_ang, n_rad, rows, cells, border)),
        out_shape=(
            jax.ShapeDtypeStruct((rows, n_theta), f32),
            jax.ShapeDtypeStruct((3, rows, n_theta), f32),
            jax.ShapeDtypeStruct((3, rows, n_theta), f32),
        ),
        in_specs=spaces,
        out_specs=[pl.BlockSpec(memory_space=pl.ANY)] * 3,
        scratch_shapes=[
            vmem((1, border), jnp.int32), vmem((1, border), jnp.int32),
            vmem((1, border), jnp.int32), vmem((4, border), f32), vmem((1, border), f32),
            vmem((FIELDS, rows, n_theta), f32), dma((3,)),
            vmem((FIELDS, LEVELS * cells, LANES), f32),
            vmem((FIELDS, LEVELS * cells, LANES), f32),
            vmem((5, cells, FIELDS, LEVELS, LANES), f32),
            vmem((cells, FIELDS, LEVELS, LANES), f32),
            vmem((cells, FIELDS, LEVELS, LANES), f32),
            vmem((cells + 2, FIELDS, LEVELS, LANES), f32),
            vmem((cells + 2, FIELDS, LEVELS, LANES), f32),
            vmem((5, LEVELS, LANES), f32),
            vmem((4, 2, FIELDS, LEVELS, LANES), f32),
            vmem((5, 2, LEVELS, LANES), f32),
            vmem((4, 2, 2, LEVELS, LANES), f32),
            vmem((4, 2 * n_ang, LEVELS, LANES), f32),
            vmem((4, sources, LEVELS, LANES), f32),
            vmem((LEVELS, LANES), f32),
            vmem((n_ang, LEVELS, LANES), f32),
            vmem((tiles, 2, cells, LANES), f32),
            vmem((tiles, 2 * LANES, 2 * LANES), jnp.bfloat16),
            dma((5,)), dma((3,)), dma((3, n_rad)), dma((3, n_rad)), dma((3, n_rad)), dma((3, n_rad)),
            dma, dma, dma((4, 2)), dma((4, 2)), dma((4, 2)), dma((4, 2)), dma((4,)), dma((4,)),
        ],
        compiler_params=pltpu.CompilerParams(
            collective_id=0, has_side_effects=True, vmem_limit_bytes=vmem_bytes
        ),
    )(
        *[pltpu.with_memory_space_constraint(x, pltpu.HBM) for x in (
        density.reshape(rows, n_theta),
        momentum.reshape(3, rows, n_theta),
        magnetic.reshape(3, rows, n_theta),
        partner_device.reshape(1, border),
        partner_phi, partner_theta,
        partner_weight.reshape(border, 4).T,
        border_turn,
        )]
    )
    outs = pl.pallas_call(
        hand_over,
        out_shape=tuple(jax.ShapeDtypeStruct(o.shape, f32) for o in outs),
        in_specs=[pl.BlockSpec(memory_space=pl.ANY)] * 3,
        out_specs=[pl.BlockSpec(memory_space=pltpu.HBM)] * 3,
        scratch_shapes=[dma((FIELDS,))],
        compiler_params=pltpu.CompilerParams(vmem_limit_bytes=vmem_bytes),
    )(*outs)
    return (
        outs[0].reshape(density.shape),
        outs[1].reshape(momentum.shape),
        outs[2].reshape(magnetic.shape),
    )


def solution(mesh):
    in_specs = (
        P("panel", "rad", "ang", None),
        P("panel", None, "rad", "ang", None),
        P("panel", None, "rad", "ang", None),
        P("panel", "ang", None),
        P("panel", "ang"),
        P("panel", "ang"),
        P("panel", "ang", None),
        P("panel", "ang"),
    )
    out_specs = (
        P("panel", "rad", "ang", None),
        P("panel", None, "rad", "ang", None),
        P("panel", None, "rad", "ang", None),
    )
    return jax.shard_map(body, mesh=mesh, in_specs=in_specs, out_specs=out_specs, check_vma=False)
```

```python
import functools
import math

import jax
import jax.numpy as jnp
from jax import lax
from jax.experimental import pallas as pl
from jax.experimental.pallas import tpu as pltpu
from jax.sharding import PartitionSpec as P

time_step = 0.15
mixing = (0.0, 0.1, 0.1, 0.1, 0.1, 0.1, 0.1)
wall = (1.0, -1.0, -1.0, -1.0, 1.0, 1.0, 1.0)
r_inner = 0.35
FIELDS = 7
LANES = 128
LEVELS = 8
vmem_bytes = 32 * 1024 * 1024
ahead = (0.5 * time_step, 0.5 * time_step, time_step)
share = (time_step / 6.0, time_step / 3.0, time_step / 3.0, time_step / 6.0)


def point_values(u):
    rate = 1.0 / u[0]
    speed = [u[1 + c] * rate for c in range(3)]
    pressure = u[0] + 0.5 * (u[4] * u[4] + u[5] * u[5] + u[6] * u[6])
    return speed, pressure


def flux_of(u, speed, pressure, d, stress, twist):
    out = [u[1 + d]]
    for c in range(3):
        key = (min(c, d), max(c, d))
        if key not in stress:
            term = u[1 + c] * speed[d] - u[4 + c] * u[4 + d]
            stress[key] = term + pressure if c == d else term
        out.append(stress[key])
    for c in range(3):
        if c == d:
            out.append(None)
            continue
        key = (min(c, d), max(c, d))
        if key not in twist:
            low, high = key
            twist[key] = speed[high] * u[4 + low] - u[4 + high] * speed[low]
        out.append(twist[key] if c == key[0] else -twist[key])
    return out


def low_high(u, flux, half, mix):
    low, high = [], []
    for f in range(FIELDS):
        carried = None if flux[f] is None else half * flux[f]
        spread = None if mixing[f] == 0.0 else mix * u[f]
        if carried is None:
            low.append(spread)
            high.append(spread)
        elif spread is None:
            low.append(carried)
            high.append(-carried)
        else:
            low.append(spread + carried)
            high.append(spread - carried)
    return low, high


def kernel(
    sizes,
    den, mom, mag, pdev_hbm, pphi_hbm, ptheta_hbm, pweight_hbm, pturn_hbm,
    oden, omom, omag,
    pdev, pphi, ptheta, pweight, pturn, first, fetch_sem,
    land, staged, state, total, slope, x_low, x_high, geo,
    phi_in, theta_out, theta_in, over_out, over_in,
    meta_out, meta_in, coef, picker,
    small_sem, own_sem, load_send, load_recv, give_send, give_recv,
    meta_send, meta_recv, phi_send, phi_recv, theta_send, theta_recv,
    over_send, over_recv,
):
    n_ang, n_rad, rows, cells, border = sizes
    side_rows = border // 2
    per_tile = LANES // border
    tiles = n_ang // per_tile
    sources = n_ang * n_rad
    mine = lax.axis_index("panel")
    a = lax.axis_index("ang")
    t = lax.axis_index("rad")
    other = 1 - mine

    def at(panel, ang, rad):
        return {"panel": panel, "ang": ang, "rad": rad}

    small = [
        pltpu.make_async_copy(src, dst, small_sem.at[i])
        for i, (src, dst) in enumerate((
            (pdev_hbm, pdev), (pphi_hbm, pphi), (ptheta_hbm, ptheta),
            (pweight_hbm, pweight), (pturn_hbm, pturn),
        ))
    ]
    for copy in small:
        copy.start()
    fetches = [
        pltpu.make_async_copy(den, first.at[0], fetch_sem.at[0]),
        pltpu.make_async_copy(mom, first.at[pl.ds(1, 3)], fetch_sem.at[1]),
        pltpu.make_async_copy(mag, first.at[pl.ds(4, 3)], fetch_sem.at[2]),
    ]
    for copy in fetches:
        copy.start()

    barrier = pltpu.get_barrier_semaphore()

    def greet(i, carry):
        pl.semaphore_signal(
            barrier, inc=1,
            device_id=at(other, i // n_rad, lax.rem(i, n_rad)),
            device_id_type=pl.DeviceIdType.MESH,
        )
        return carry

    lax.fori_loop(0, sources, greet, 0)
    for step in range(1, n_rad):
        pl.semaphore_signal(
            barrier, inc=1, device_id=at(mine, a, lax.rem(t + step, n_rad)),
            device_id_type=pl.DeviceIdType.MESH,
        )

    @pl.when(a > 0)
    def _():
        pl.semaphore_signal(
            barrier, inc=1, device_id=at(mine, a - 1, t), device_id_type=pl.DeviceIdType.MESH
        )

    @pl.when(a < n_ang - 1)
    def _():
        pl.semaphore_signal(
            barrier, inc=1, device_id=at(mine, a + 1, t), device_id_type=pl.DeviceIdType.MESH
        )

    own_rows = pl.ds(pl.multiple_of(t * rows, rows), rows)
    own_lanes = pl.ds(pl.multiple_of(t * LANES, LANES), LANES)
    own = [
        pltpu.make_async_copy(den.at[:, own_lanes], land.at[0, own_rows, :], own_sem.at[0]),
        pltpu.make_async_copy(mom.at[:, :, own_lanes], land.at[pl.ds(1, 3), own_rows, :], own_sem.at[1]),
        pltpu.make_async_copy(mag.at[:, :, own_lanes], land.at[pl.ds(4, 3), own_rows, :], own_sem.at[2]),
    ]
    for copy in own:
        copy.start()

    sub8 = lax.broadcasted_iota(jnp.int32, (LEVELS, LANES), 0)
    lane8 = lax.broadcasted_iota(jnp.int32, (LEVELS, LANES), 1)
    sub_b = lax.broadcasted_iota(jnp.int32, (border, LANES), 0)
    lane_b = lax.broadcasted_iota(jnp.int32, (border, LANES), 1)
    square = (
        lax.broadcasted_iota(jnp.int32, (border, border), 0)
        == lax.broadcasted_iota(jnp.int32, (border, border), 1)
    )

    def column(row):
        wide = jnp.broadcast_to(row, (border, border))
        return jnp.sum(jnp.where(square, wide, 0.0), axis=1, keepdims=True)

    spot_b = jnp.where(sub_b < side_rows, 2 * sub_b, 2 * sub_b - (border - 1))
    place = lane_b == spot_b + border * lax.rem(a, per_tile)
    for copy in small:
        copy.wait()
    columns = [
        column(pdev[...].astype(jnp.float32)),
        column(pphi[...].astype(jnp.float32)),
        column(ptheta[...].astype(jnp.float32)),
    ] + [column(pweight[i:i + 1, :]) for i in range(4)]
    meta_out[...] = jnp.zeros_like(meta_out)
    for i, col in enumerate(columns):
        meta_out[i:i + 1, :] = jnp.sum(
            jnp.where(place, jnp.broadcast_to(col, (border, LANES)), 0.0), axis=0, keepdims=True
        )

    at_low = t == 0
    at_high = t == n_rad - 1
    shifted = jnp.where(spot_b % 2 == 0, spot_b, lax.rem(spot_b + LANES - 2, LANES))
    ghosted = jnp.where(shifted % 2 == 0, at_low.astype(jnp.int32), at_high.astype(jnp.int32))
    turn_at = (lane_b == shifted) & (ghosted == 1)
    angle = jnp.sum(
        jnp.where(turn_at, jnp.broadcast_to(column(pturn[...]), (border, LANES)), 0.0),
        axis=0, keepdims=True,
    )
    angle = jnp.broadcast_to(angle, (LEVELS, LANES))
    cosine, sine = jnp.cos(angle), jnp.sin(angle)

    radius = r_inner + (sub8.astype(jnp.float32) + 0.5) * ((1.0 - r_inner) / LEVELS)
    theta = math.pi / 4 + ((lane8 + t * LANES).astype(jnp.float32) + 0.5) * (
        math.pi / 2 / (LANES * n_rad)
    )
    inv_radius = 1.0 / radius
    inv_both = inv_radius / jnp.sin(theta)
    half_t = 0.5 * inv_radius
    mix_t = 0.1 * inv_radius * inv_radius
    half_p = 0.5 * inv_both
    mix_p = 0.1 * inv_both * inv_both
    centre = -2.0 * (0.1 + mix_t + mix_p)
    for i, value in enumerate((half_t, mix_t, half_p, mix_p, centre)):
        geo[i] = value

    pl.semaphore_wait(
        barrier,
        sources + n_rad - 1 + jnp.where(a > 0, 1, 0) + jnp.where(a < n_ang - 1, 1, 0),
    )

    for copy in fetches:
        copy.wait()
    loads = []
    for step in range(1, n_rad):
        to = lax.rem(t + step, n_rad)
        lanes = pl.ds(pl.multiple_of(to * LANES, LANES), LANES)
        for i, (src, dst) in enumerate((
            (first.at[0, :, lanes], land.at[0, own_rows, :]),
            (first.at[pl.ds(1, 3), :, lanes], land.at[pl.ds(1, 3), own_rows, :]),
            (first.at[pl.ds(4, 3), :, lanes], land.at[pl.ds(4, 3), own_rows, :]),
        )):
            loads.append(pltpu.make_async_remote_copy(
                src_ref=src, dst_ref=dst,
                send_sem=load_send.at[i, step], recv_sem=load_recv.at[i, step],
                device_id=at(mine, a, to), device_id_type=pl.DeviceIdType.MESH,
            ))
    for copy in loads:
        copy.start()

    def meta_copy(to):
        return pltpu.make_async_remote_copy(
            src_ref=meta_out, dst_ref=meta_in.at[a],
            send_sem=meta_send, recv_sem=meta_recv,
            device_id=at(other, to, t), device_id_type=pl.DeviceIdType.MESH,
        )

    def send_meta(to, carry):
        meta_copy(to).start()
        return carry

    lax.fori_loop(0, n_ang, send_meta, 0)
    pltpu.make_async_copy(meta_in, meta_in, meta_recv).wait()

    sub_l = lax.broadcasted_iota(jnp.int32, (LANES, LANES), 0)
    sub_c = lax.broadcasted_iota(jnp.int32, (cells, LANES), 0)

    def prepare(g, carry):
        table = jnp.sum(meta_in[pl.ds(g * per_tile, per_tile)], axis=0)
        device = table[0:1].astype(jnp.int32)
        at_phi = table[1:2].astype(jnp.int32)
        at_theta = table[2:3].astype(jnp.int32) - t * LANES
        hit = jnp.broadcast_to(device == a, (cells, LANES))
        near = hit & (sub_c == at_phi)
        far = hit & (sub_c == at_phi + 1)
        zero = jnp.zeros((cells, LANES), jnp.float32)
        w = [jnp.broadcast_to(table[3 + i:4 + i], (cells, LANES)) for i in range(4)]
        coef[g, 0] = jnp.where(near, w[0], jnp.where(far, w[2], zero))
        coef[g, 1] = jnp.where(near, w[1], jnp.where(far, w[3], zero))
        first = jnp.where(sub_l == at_theta, 1.0, 0.0).astype(jnp.bfloat16)
        second = jnp.where(sub_l == at_theta + 1, 1.0, 0.0).astype(jnp.bfloat16)
        for part in range(2):
            picker[g, pl.ds(part * LANES, LANES), pl.ds(0, LANES)] = first
            picker[g, pl.ds(part * LANES, LANES), pl.ds(LANES, LANES)] = second
        return carry

    if tiles == 1:
        prepare(0, 0)
    else:
        lax.fori_loop(0, tiles, prepare, 0)

    for copy in own:
        copy.wait()
    for copy in loads:
        copy.wait_recv()

    block_of = lane8 // border
    pair8 = lane8 // 2
    even = lane8 % 2 == 0
    first_lane = lane8 == 0
    last_lane = lane8 == LANES - 1
    first_level = sub8 == 0
    last_level = sub8 == LEVELS - 1

    def pack(k, f, value, packs):
        spot = border * (f % per_tile) + 2 * k + 1
        hit = pair8 == border // 2 * (f % per_tile) + k
        packs[f // per_tile] = jnp.where(
            hit, pltpu.roll(value, lax.rem(spot, LANES), 1), packs[f // per_tile]
        )

    def phi_copies(s):
        down = pltpu.make_async_remote_copy(
            src_ref=state.at[s, 0], dst_ref=phi_in.at[s, 1],
            send_sem=phi_send.at[s, 0], recv_sem=phi_recv.at[s, 1],
            device_id=at(mine, a, t) | {"ang": jnp.maximum(a - 1, 0)},
            device_id_type=pl.DeviceIdType.MESH,
        )
        up = pltpu.make_async_remote_copy(
            src_ref=state.at[s, cells - 1], dst_ref=phi_in.at[s, 0],
            send_sem=phi_send.at[s, 1], recv_sem=phi_recv.at[s, 0],
            device_id=at(mine, a, t) | {"ang": jnp.minimum(a + 1, n_ang - 1)},
            device_id_type=pl.DeviceIdType.MESH,
        )
        return down, up

    def theta_copies(s):
        down = pltpu.make_async_remote_copy(
            src_ref=theta_out.at[s], dst_ref=theta_in.at[s, 1],
            send_sem=theta_send.at[s, 0], recv_sem=theta_recv.at[s, 1],
            device_id=at(mine, a, jnp.maximum(t - 1, 0)),
            device_id_type=pl.DeviceIdType.MESH,
        )
        up = pltpu.make_async_remote_copy(
            src_ref=theta_out.at[s], dst_ref=theta_in.at[s, 0],
            send_sem=theta_send.at[s, 1], recv_sem=theta_recv.at[s, 0],
            device_id=at(mine, a, jnp.minimum(t + 1, n_rad - 1)),
            device_id_type=pl.DeviceIdType.MESH,
        )
        return down, up

    def over_copy(s, q):
        return pltpu.make_async_remote_copy(
            src_ref=over_out.at[s, q], dst_ref=over_in.at[s, a * n_rad + t],
            send_sem=over_send.at[s], recv_sem=over_recv.at[s],
            device_id=at(other, q // 2, lax.rem(q, 2) * (n_rad - 1)),
            device_id_type=pl.DeviceIdType.MESH,
        )

    def send_all(s):
        theta_down, theta_up = theta_copies(s)
        phi_down, phi_up = phi_copies(s)
        for can, copy in (
            (t > 0, theta_down), (t < n_rad - 1, theta_up),
            (a > 0, phi_down), (a < n_ang - 1, phi_up),
        ):
            pl.when(can)(copy.start)

        def overset(g, carry):
            value = state[s].reshape(cells * FIELDS * LEVELS, LANES)
            head = value.astype(jnp.bfloat16)
            rest = (value - head.astype(jnp.float32)).astype(jnp.bfloat16)
            got = jnp.dot(
                jnp.concatenate([head, rest], axis=1), picker[g],
                preferred_element_type=jnp.float32,
            )
            ghosts = [None] * FIELDS
            for k in range(cells):
                near = jnp.broadcast_to(coef[g, 0, k:k + 1, :], (LEVELS, LANES))
                far = jnp.broadcast_to(coef[g, 1, k:k + 1, :], (LEVELS, LANES))
                for f in range(FIELDS):
                    at_row = (k * FIELDS + f) * LEVELS
                    piece = got[at_row:at_row + LEVELS]
                    term = piece[:, :LANES] * near + piece[:, LANES:] * far
                    ghosts[f] = term if k == 0 else ghosts[f] + term
            turned = [
                pltpu.roll(ghosts[f], border * (f % per_tile), 1) if f % per_tile else ghosts[f]
                for f in range(FIELDS)
            ]
            for j in range(per_tile):
                pair = []
                for half in range(2):
                    members = range(half * per_tile, min(FIELDS, (half + 1) * per_tile))
                    message = turned[members[0]]
                    for f in members:
                        message = jnp.where(
                            block_of == (f + j) % per_tile, turned[f], message
                        )
                    if j:
                        message = pltpu.roll(message, LANES - j * border, 1)
                    pair.append(message)
                at_pair = 2 * (g * per_tile + j)
                over_out[s, at_pair] = jnp.where(even, pair[0], pltpu.roll(pair[1], 1, 1))
                over_out[s, at_pair + 1] = jnp.where(
                    even, pltpu.roll(pair[0], LANES - 1, 1), pair[1]
                )
            for j in range(2 * per_tile):
                over_copy(s, g * 2 * per_tile + j).start()
            return carry

        if tiles == 1:
            overset(0, 0)
        else:
            lax.fori_loop(0, tiles, overset, 0)

    def inner(s):
        half_t, mix_t, half_p, mix_p, centre = [geo[i] for i in range(5)]

        def row(k, carry):
            u = [state[s, k, f] for f in range(FIELDS)]
            speed, pressure = point_values(u)
            stress, twist = {}, {}
            low_r, high_r = low_high(u, flux_of(u, speed, pressure, 0, stress, twist), 0.5, 0.1)
            low_t, high_t = low_high(u, flux_of(u, speed, pressure, 1, stress, twist), half_t, mix_t)
            low_p, high_p = low_high(u, flux_of(u, speed, pressure, 2, stress, twist), half_p, mix_p)
            for f in range(FIELDS):
                below = pltpu.roll(low_r[f], 1, 0)
                above = pltpu.roll(high_r[f], LEVELS - 1, 0)
                below = jnp.where(first_level, wall[f] * high_r[f], below)
                above = jnp.where(last_level, wall[f] * low_r[f], above)
                left = jnp.where(first_lane, 0.0, pltpu.roll(low_t[f], 1, 1))
                right = jnp.where(last_lane, 0.0, pltpu.roll(high_t[f], LANES - 1, 1))
                value = (below + above) + (left + right)
                if mixing[f] != 0.0:
                    value = value + centre * u[f]
                slope[k, f] = value
                x_low[k + 1, f] = low_p[f]
                x_high[k + 1, f] = high_p[f]
            return carry

        lax.fori_loop(0, cells, row, 0, unroll=True)

    def halos(s):
        half_t, mix_t, half_p, mix_p, centre = [geo[i] for i in range(5)]
        phi_down, phi_up = phi_copies(s)
        theta_down, theta_up = theta_copies(s)

        def beside(side):
            u = [phi_in[s, side, f] for f in range(FIELDS)]
            speed, pressure = point_values(u)
            low, high = low_high(u, flux_of(u, speed, pressure, 2, {}, {}), half_p, mix_p)
            for f in range(FIELDS):
                if side == 0:
                    x_low[0, f] = low[f]
                else:
                    x_high[cells + 1, f] = high[f]

        @pl.when(a > 0)
        def _():
            phi_up.wait_recv()
            beside(0)

        @pl.when(a == 0)
        def _():
            for f in range(FIELDS):
                x_low[0, f] = wall[f] * x_high[1, f]

        @pl.when(a < n_ang - 1)
        def _():
            phi_down.wait_recv()
            beside(1)

        @pl.when(a == n_ang - 1)
        def _():
            for f in range(FIELDS):
                x_high[cells + 1, f] = wall[f] * x_low[cells, f]

        @pl.when(t > 0)
        def _():
            theta_up.wait_recv()

        @pl.when(t < n_rad - 1)
        def _():
            theta_down.wait_recv()

        @pl.when(at_low | at_high)
        def _():
            pltpu.make_async_copy(over_in.at[s], over_in.at[s], over_recv.at[s]).wait()
            ghost = jnp.sum(over_in[s], axis=0)
            @pl.when(at_low)
            def _():
                theta_in[s, 0, 0] = ghost
                theta_in[s, 0, 1] = pltpu.roll(ghost, LANES - 1, 1)

            @pl.when(at_high)
            def _():
                theta_in[s, 1, 0] = pltpu.roll(ghost, 1, 1)
                theta_in[s, 1, 1] = ghost

        both = [
            jnp.where(even, theta_in[s, 0, h], pltpu.roll(theta_in[s, 1, h], LANES - 2, 1))
            for h in range(2)
        ]
        u = []
        for f in range(FIELDS):
            away = border * (f % per_tile)
            value = both[f // per_tile]
            u.append(pltpu.roll(value, LANES - away, 1) if away else value)
        for f in (2, 5):
            u[f], u[f + 1] = cosine * u[f] + sine * u[f + 1], cosine * u[f + 1] - sine * u[f]
        speed, pressure = point_values(u)
        signed = jnp.where(even, half_t, -half_t)
        edge, _ = low_high(u, flux_of(u, speed, pressure, 1, {}, {}), signed, mix_t)
        return edge

    def tend(k, f, edge):
        ends = pltpu.roll(edge[f], lax.rem(LANES - 2 * k, LANES), 1)
        ends = jnp.where(outer_lanes, ends, 0.0)
        return (slope[k, f] + ends) + (x_low[k, f] + x_high[k + 2, f])

    zero8 = jnp.zeros((LEVELS, LANES), jnp.float32)
    outer_lanes = first_lane | last_lane

    def enter(k, packs):
        packs = list(packs)
        for f in range(FIELDS):
            value = land[f, pl.ds(k, LEVELS, stride=cells), :]
            state[0, k, f] = value
            total[k, f] = value
            pack(k, f, value, packs)
        return tuple(packs)

    def keep(s, packs):
        for half in range(2):
            theta_out[s, half] = packs[half]

    keep(0, lax.fori_loop(0, cells, enter, (zero8, zero8), unroll=True))

    def stage(s, carry):
        send_all(s)
        inner(s)
        edge = halos(s)
        step_on = jnp.where(s < 2, ahead[0], ahead[2])
        weight = jnp.where((s == 0) | (s == 3), share[0], share[1])

        def advance(k, packs):
            packs = list(packs)
            for f in range(FIELDS):
                now = tend(k, f, edge)
                value = state[0, k, f] + step_on * now
                state[s + 1, k, f] = value
                pack(k, f, value, packs)
                total[k, f] = total[k, f] + weight * now
            return tuple(packs)

        keep(s + 1, lax.fori_loop(0, cells, advance, (zero8, zero8), unroll=True))
        return carry

    lax.fori_loop(0, 4, stage, 0)

    def leave(fields):
        def move(k, carry):
            for f in fields:
                staged[f, pl.ds(k, LEVELS, stride=cells), :] = total[k, f]
            return carry

        lax.fori_loop(0, cells, move, 0, unroll=True)

    gives = []
    for step in range(1, n_rad):
        to = lax.rem(t + step, n_rad)
        there = pl.ds(pl.multiple_of(to * rows, rows), rows)
        for i, (src, dst) in enumerate((
            (staged.at[0, there, :], oden.at[:, own_lanes]),
            (staged.at[pl.ds(1, 3), there, :], omom.at[:, :, own_lanes]),
            (staged.at[pl.ds(4, 3), there, :], omag.at[:, :, own_lanes]),
        )):
            gives.append(pltpu.make_async_remote_copy(
                src_ref=src, dst_ref=dst,
                send_sem=give_send.at[i, step], recv_sem=give_recv.at[i, step],
                device_id=at(mine, a, to), device_id_type=pl.DeviceIdType.MESH,
            ))
    for i, fields in enumerate(((0,), (1, 2, 3), (4, 5, 6))):
        leave(fields)
        for copy in gives[i::3]:
            copy.start()
    keeps = [
        pltpu.make_async_copy(staged.at[0, own_rows, :], oden.at[:, own_lanes], own_sem.at[0]),
        pltpu.make_async_copy(staged.at[pl.ds(1, 3), own_rows, :], omom.at[:, :, own_lanes], own_sem.at[1]),
        pltpu.make_async_copy(staged.at[pl.ds(4, 3), own_rows, :], omag.at[:, :, own_lanes], own_sem.at[2]),
    ]
    for copy in keeps:
        copy.start()

    for copy in loads:
        copy.wait_send()
    pltpu.make_async_copy(meta_in, meta_in, meta_send).wait()
    for s in range(4):
        phi_down, phi_up = phi_copies(s)
        theta_down, theta_up = theta_copies(s)
        for can, copy in (
            (t > 0, theta_down), (t < n_rad - 1, theta_up),
            (a > 0, phi_down), (a < n_ang - 1, phi_up),
        ):
            pl.when(can)(copy.wait_send)
        pltpu.make_async_copy(over_out.at[s], over_out.at[s], over_send.at[s]).wait()
    for copy in keeps:
        copy.wait()
    for copy in gives:
        copy.wait()


def hand_over(one, two, three, out_one, out_two, out_three, sems):
    copies = [
        pltpu.make_async_copy(src, dst, sems.at[i])
        for i, (src, dst) in enumerate(
            [(one, out_one)]
            + [(two.at[c], out_two.at[c]) for c in range(3)]
            + [(three.at[c], out_three.at[c]) for c in range(3)]
        )
    ]
    for copy in copies:
        copy.start()
    for copy in copies:
        copy.wait()


def body(density, momentum, magnetic, partner_device, partner_phi, partner_theta, partner_weight,
         border_turn):
    _, rows_r, cells, n_theta = density.shape
    border = partner_phi.shape[1]
    n_ang, n_rad = lax.axis_size("ang"), lax.axis_size("rad")
    rows = rows_r * cells
    assert rows_r * n_rad == LEVELS and n_theta == LANES * n_rad and n_rad > 1
    assert border * 4 == LANES and n_ang % (LANES // border) == 0 and border == 2 * cells
    f32 = jnp.float32
    tiles = n_ang * border // LANES
    sources = n_ang * n_rad
    vmem = pltpu.VMEM
    dma = pltpu.SemaphoreType.DMA
    spaces = [pl.BlockSpec(memory_space=pltpu.HBM)] * 8
    outs = pl.pallas_call(
        functools.partial(kernel, (n_ang, n_rad, rows, cells, border)),
        out_shape=(
            jax.ShapeDtypeStruct((rows, n_theta), f32),
            jax.ShapeDtypeStruct((3, rows, n_theta), f32),
            jax.ShapeDtypeStruct((3, rows, n_theta), f32),
        ),
        in_specs=spaces,
        out_specs=[pl.BlockSpec(memory_space=pl.ANY)] * 3,
        scratch_shapes=[
            vmem((1, border), jnp.int32), vmem((1, border), jnp.int32),
            vmem((1, border), jnp.int32), vmem((4, border), f32), vmem((1, border), f32),
            vmem((FIELDS, rows, n_theta), f32), dma((3,)),
            vmem((FIELDS, LEVELS * cells, LANES), f32),
            vmem((FIELDS, LEVELS * cells, LANES), f32),
            vmem((5, cells, FIELDS, LEVELS, LANES), f32),
            vmem((cells, FIELDS, LEVELS, LANES), f32),
            vmem((cells, FIELDS, LEVELS, LANES), f32),
            vmem((cells + 2, FIELDS, LEVELS, LANES), f32),
            vmem((cells + 2, FIELDS, LEVELS, LANES), f32),
            vmem((5, LEVELS, LANES), f32),
            vmem((4, 2, FIELDS, LEVELS, LANES), f32),
            vmem((5, 2, LEVELS, LANES), f32),
            vmem((4, 2, 2, LEVELS, LANES), f32),
            vmem((4, 2 * n_ang, LEVELS, LANES), f32),
            vmem((4, sources, LEVELS, LANES), f32),
            vmem((LEVELS, LANES), f32),
            vmem((n_ang, LEVELS, LANES), f32),
            vmem((tiles, 2, cells, LANES), f32),
            vmem((tiles, 2 * LANES, 2 * LANES), jnp.bfloat16),
            dma((5,)), dma((3,)), dma((3, n_rad)), dma((3, n_rad)), dma((3, n_rad)), dma((3, n_rad)),
            dma, dma, dma((4, 2)), dma((4, 2)), dma((4, 2)), dma((4, 2)), dma((4,)), dma((4,)),
        ],
        compiler_params=pltpu.CompilerParams(
            collective_id=0, has_side_effects=True, vmem_limit_bytes=vmem_bytes
        ),
    )(
        *[pltpu.with_memory_space_constraint(x, pltpu.HBM) for x in (
        density.reshape(rows, n_theta),
        momentum.reshape(3, rows, n_theta),
        magnetic.reshape(3, rows, n_theta),
        partner_device.reshape(1, border),
        partner_phi, partner_theta,
        partner_weight.reshape(border, 4).T,
        border_turn,
        )]
    )
    outs = pl.pallas_call(
        hand_over,
        out_shape=tuple(jax.ShapeDtypeStruct(o.shape, f32) for o in outs),
        in_specs=[pl.BlockSpec(memory_space=pl.ANY)] * 3,
        out_specs=[pl.BlockSpec(memory_space=pltpu.HBM)] * 3,
        scratch_shapes=[dma((FIELDS,))],
        compiler_params=pltpu.CompilerParams(vmem_limit_bytes=vmem_bytes),
    )(*outs)
    return (
        outs[0].reshape(density.shape),
        outs[1].reshape(momentum.shape),
        outs[2].reshape(magnetic.shape),
    )


def solution(mesh):
    in_specs = (
        P("panel", "rad", "ang", None),
        P("panel", None, "rad", "ang", None),
        P("panel", None, "rad", "ang", None),
        P("panel", "ang", None),
        P("panel", "ang"),
        P("panel", "ang"),
        P("panel", "ang", None),
        P("panel", "ang"),
    )
    out_specs = (
        P("panel", "rad", "ang", None),
        P("panel", None, "rad", "ang", None),
        P("panel", None, "rad", "ang", None),
    )
    return jax.shard_map(body, mesh=mesh, in_specs=in_specs, out_specs=out_specs, check_vma=False)
```
